32 devices in a mesh: dp: 4 (over y, x), space: 8 (over z, core).
Axes of the slice: x: 2, y: 2, z: 4, core: 2. Of those that a mesh axis runs over, the one named last changes fastest.
Arguments:
- images: bfloat16 [4, 64, 64, 1536], P('dp', 'space'), may hold values from -8 to 8
- dw_kernel: bfloat16 [7, 7, 1536], replicated, may hold values from -0.875 to 0.875
- dw_bias: float32 [1536], replicated, may hold values from -3 to 3
- ln_gain: float32 [1536], replicated, may hold values from 0.1 to 1.9
- ln_shift: float32 [1536], replicated, may hold values from -2 to 2
- proj: bfloat16 [1536, 1024], replicated, may hold values from -0.15625 to 0.15625
- text: float32 [4, 1024], P('dp'), may hold values from -6 to 6
- logit_scale: float32 [1], replicated, may hold values from 10 to 100
Outputs:
- loss: float32 [], replicated
- grad_images: bfloat16 [4, 64, 64, 1536], P('dp', 'space')
- kernel_grad: float32 [7, 7, 1536], replicated
- text_grad: float32 [4, 1024], P('dp')
The draws below stay inside these ranges and needn't reach their ends.
All inputs are finite; a program needn't handle non-finite values.
Results may differ from the reference program's by a relative error of at most 0.0013.
Values may be sent and summed in bfloat16 or wider, within the bound.
A program may use at most 128 MiB of HBM per device.

```python
import jax
import jax.numpy as jnp
from jax import lax

CHANNELS = 1536
EMBED = 1024
KERNEL = 7
WIDTH = 64
BATCH = 4
HEIGHT = 64


def draw_images(key, part):
    first, second, third = jax.random.split(key, 3)
    offsets = jax.random.normal(first, (BATCH, 1, 1, CHANNELS), jnp.float32)
    channel_scale = jnp.exp(jax.random.uniform(third, (1, 1, 1, CHANNELS), jnp.float32, -1.2, 1.2))
    noise = jax.random.normal(second, (BATCH, HEIGHT, WIDTH, CHANNELS), jnp.float32)
    row_amp = 1.0 + 2.0 * jnp.arange(HEIGHT, dtype=jnp.float32) / HEIGHT
    image_amp = 1.0 + 2.0 * jnp.arange(BATCH, dtype=jnp.float32) / BATCH
    amplitude = row_amp[None, :, None, None] * image_amp[:, None, None, None]
    values = amplitude * (0.8 * offsets + 0.5 * noise * channel_scale)
    return jnp.clip(values, -8.0, 8.0).astype(jnp.bfloat16)


def draw_logit_scale(key, part):
    return jax.random.uniform(key, (1,), jnp.float32, 10.0, 30.0)


def level_of(rng, shape, shards, smallest, top_value):
    def one(dim, shards_of):
        heights = jax.random.uniform(jax.random.fold_in(jax.random.fold_in(rng, 6), dim), (shards_of,), jnp.float32, smallest / len(shards), top_value / len(shards))
        return jnp.repeat(jnp.exp(heights), shape[dim] // shards_of).reshape((-1,) + (1,) * (len(shape) - dim - 1))

    level = one(*shards[0])
    for cut in shards[1:]:
        level = level * one(*cut)
    return level


def scatter_about(key, extent, width, limit, shards=(), held_as=jnp.bfloat16):
    values = width * jax.random.normal(key, extent, jnp.float32)
    if shards:
        values = values * level_of(key, extent, shards, -0.22, 0.18)
    return jnp.clip(values, -limit, limit).astype(held_as)


def setup_inputs(seed: int = 0) -> dict:
    key_of = jax.random.split(jax.random.key(seed), 9)
    return {
        "images": draw_images(jax.random.fold_in(key_of[8], 71), 0),
        "dw_kernel": scatter_about(key_of[1], (KERNEL, KERNEL, CHANNELS), (KERNEL * KERNEL) ** -0.5, 0.875),
        "dw_bias": scatter_about(key_of[2], (CHANNELS,), 0.5, 3.0, (), jnp.float32),
        "ln_gain": jnp.clip(1.0 + 0.18 * jax.random.normal(key_of[3], (CHANNELS,), jnp.float32), 0.1, 1.9),
        "ln_shift": scatter_about(key_of[4], (CHANNELS,), 0.3, 2.0, (), jnp.float32),
        "proj": scatter_about(key_of[5], (CHANNELS, EMBED), CHANNELS ** -0.5, 0.15625),
        "text": scatter_about(key_of[6], (BATCH, EMBED), 1.0, 6.0, ((0, 4),), jnp.float32),
        "logit_scale": draw_logit_scale(jax.random.fold_in(key_of[8], 71), 0),
    }


def normalize(values):
    centre_value = lax.optimization_barrier(jnp.mean(values, axis=-1, keepdims=True))
    centred = values - centre_value
    spread = lax.optimization_barrier(jnp.mean(centred * centred, axis=-1, keepdims=True))
    inv_dev = lax.rsqrt(spread + 1e-06)
    return (centred * inv_dev, inv_dev)

def convolve(padded, kernel_float, row_count, col_count):
    result = jnp.zeros((row_count, col_count, padded.shape[-1]), jnp.float32)
    for a in range(kernel_float.shape[0]):
        for d in range(kernel_float.shape[1]):
            result = result + padded[a:a + row_count, d:d + col_count, :] * kernel_float[a, d]
    return result

def logsum(scores, axis):
    highest = lax.optimization_barrier(jnp.max(scores, axis=axis, keepdims=True))
    return jnp.squeeze(highest, axis) + jnp.log(lax.optimization_barrier(jnp.sum(jnp.exp(scores - highest), axis=axis)))

def reference(images, dw_kernel, dw_bias, ln_gain, ln_shift, proj, text, logit_scale):
    reach_rows = KERNEL // 2
    kernel_float = dw_kernel.astype(jnp.float32)
    row_count = images.shape[1]
    col_count = images.shape[2]
    pixel_count = row_count * col_count

    def forward_one(single_image):
        padded = jnp.pad(single_image.astype(jnp.float32), ((reach_rows, reach_rows), (reach_rows, reach_rows), (0, 0)))
        conv_out = convolve(padded, kernel_float, row_count, col_count) + dw_bias
        normed, inv_dev = normalize(conv_out)
        return lax.optimization_barrier(jnp.sum(normed * ln_gain + ln_shift, axis=(0, 1))) / pixel_count
    pooled = lax.map(forward_one, images)
    proj_float = proj.astype(jnp.float32)
    embedded = jnp.dot(pooled, proj_float, precision=lax.Precision.HIGHEST)
    emb_norm = jnp.sqrt(lax.optimization_barrier(jnp.sum(embedded * embedded, axis=-1, keepdims=True)))
    unit_img = embedded / emb_norm
    text_norm = jnp.sqrt(lax.optimization_barrier(jnp.sum(text * text, axis=-1, keepdims=True)))
    unit_txt = text / text_norm
    factor = logit_scale[0]
    scores = factor * jnp.dot(unit_img, unit_txt.T, precision=lax.Precision.HIGHEST)
    row_logsum = logsum(scores, 1)
    col_logsum = logsum(scores, 0)
    diagonal = jnp.diagonal(scores)
    batch_count = scores.shape[0]
    loss = (jnp.sum(row_logsum - diagonal) + jnp.sum(col_logsum - diagonal)) / (2 * batch_count)
    identity = jnp.eye(batch_count, dtype=jnp.float32)
    score_grad = 0.5 * (jnp.exp(scores - row_logsum[:, None]) + jnp.exp(scores - col_logsum[None, :])) - identity
    unit_img_grad = factor * jnp.dot(score_grad, unit_txt, precision=lax.Precision.HIGHEST)
    unit_txt_grad = factor * jnp.dot(score_grad.T, unit_img, precision=lax.Precision.HIGHEST)
    text_grad = (unit_txt_grad - unit_txt * lax.optimization_barrier(jnp.sum(unit_txt * unit_txt_grad, axis=-1, keepdims=True))) / text_norm
    emb_grad = (unit_img_grad - unit_img * lax.optimization_barrier(jnp.sum(unit_img * unit_img_grad, axis=-1, keepdims=True))) / emb_norm
    weighted = jnp.dot(emb_grad, proj_float.T, precision=lax.Precision.HIGHEST) * ln_gain

    def backward_one(inputs):
        single_image, weight_row = inputs
        padded = jnp.pad(single_image.astype(jnp.float32), ((reach_rows, reach_rows), (reach_rows, reach_rows), (0, 0)))
        conv_out = convolve(padded, kernel_float, row_count, col_count) + dw_bias
        normed, inv_dev = normalize(conv_out)
        weight_mean = jnp.mean(weight_row)
        spread_term = lax.optimization_barrier(jnp.mean(weight_row * normed, axis=-1, keepdims=True))
        pixel_grad = inv_dev * (weight_row - weight_mean - normed * spread_term)
        grad_pad = jnp.pad(pixel_grad, ((reach_rows, reach_rows), (reach_rows, reach_rows), (0, 0)))
        input_grad = jnp.zeros_like(pixel_grad)
        for a in range(KERNEL):
            for d in range(KERNEL):
                start_row = 2 * reach_rows - a
                start_col = 2 * reach_rows - d
                input_grad = input_grad + kernel_float[a, d] * grad_pad[start_row:start_row + row_count, start_col:start_col + col_count, :]
        kernel_terms = jnp.stack([jnp.stack([lax.optimization_barrier(jnp.sum(pixel_grad * padded[a:a + row_count, d:d + col_count, :], axis=(0, 1))) for d in range(KERNEL)]) for a in range(KERNEL)])
        return (input_grad.astype(jnp.bfloat16), kernel_terms)
    grad_images, kernel_terms = lax.map(backward_one, (images, weighted))
    kernel_grad = lax.optimization_barrier(jnp.sum(kernel_terms, axis=0)) / pixel_count
    return (loss, grad_images, kernel_grad, text_grad)
```

```python
import functools

import jax
import jax.numpy as jnp
from jax import lax
from jax.experimental import pallas as pl
from jax.experimental.pallas import tpu as pltpu
from jax.sharding import PartitionSpec as P

LANES = 128
PAD = 8
TILE = 32
VMEM_LIMIT = 50 * 1024 * 1024
MESH = pl.DeviceIdType.MESH


def fill_taps(taps_ref, k_ref):
    for i in range(k_ref.shape[0]):
        taps_ref[i] = jnp.broadcast_to(k_ref[i : i + 1, :], taps_ref.shape[1:])


def fill_padded(pad_ref, low_ref, x_ref, high_ref):
    cols = x_ref.shape[1]
    first = 0
    for part in (low_ref, x_ref, high_ref):
        count = part.shape[0]
        pad_ref[first : first + count, PAD : PAD + cols, :] = part[...].astype(jnp.float32)
        first += count


def clear_edges(pad_ref, cols):
    rows = pad_ref.shape[0]
    zeros = jnp.zeros((rows, PAD, LANES), jnp.float32)
    pad_ref[:, 0:PAD, :] = zeros
    pad_ref[:, PAD + cols : PAD + cols + PAD, :] = zeros


def convolve(pad_ref, taps_ref, side, rows, start, flip):
    reach = side // 2
    acc = [None] * rows
    for r in range(rows + side - 1):
        for d in range(side):
            first = PAD - reach + d + start
            x = pad_ref[r, first : first + TILE, :].reshape(TILE // 8, 8, LANES)
            for a in range(side):
                h = r - a
                if 0 <= h < rows:
                    tap = (side - 1 - a) * side + side - 1 - d if flip else a * side + d
                    product = x * taps_ref[tap][None]
                    acc[h] = product if acc[h] is None else acc[h] + product
    return acc


def forward_kernel(side, low_ref, x_ref, high_ref, k_ref, bias_ref, gain_ref, shift_ref,
                   normed_ref, inv_ref, pool_ref, pad_ref, taps_ref, sums_ref):
    step = pl.program_id(0)
    blocks, rows, cols, _ = normed_ref.shape
    channels = blocks * LANES
    fill_taps(taps_ref, k_ref)
    clear_edges(pad_ref, cols)
    fill_padded(pad_ref, low_ref, x_ref, high_ref)
    for start in range(0, cols, TILE):
        acc = convolve(pad_ref, taps_ref, side, rows, start, False)
        for h in range(rows):
            normed_ref[step, h, start : start + TILE, :] = (
                acc[h].reshape(TILE, LANES) + bias_ref[...]
            )

    @pl.when(step == blocks - 1)
    def _():
        sums_ref[...] = jnp.zeros_like(sums_ref)

        def one_row(h, carry):
            total = normed_ref[0, h]
            for b in range(1, blocks):
                total = total + normed_ref[b, h]
            mu = jnp.sum(total, axis=1, keepdims=True) / channels
            mu = jnp.broadcast_to(mu, (cols, LANES))
            total = None
            for b in range(blocks):
                centred = normed_ref[b, h] - mu
                total = centred * centred if total is None else total + centred * centred
            spread = jnp.sum(total, axis=1, keepdims=True) / channels
            inv = jnp.broadcast_to(lax.rsqrt(spread + 1e-6), (cols, LANES))
            inv_ref[h] = inv
            for b in range(blocks):
                normed = (normed_ref[b, h] - mu) * inv
                normed_ref[b, h] = normed
                sums_ref[b] += jnp.sum(normed.reshape(cols // 8, 8, LANES), axis=0)
            return carry

        lax.fori_loop(0, rows, one_row, 0)
        for b in range(blocks):
            span = slice(b * LANES, (b + 1) * LANES)
            pool_ref[:, span] = (
                jnp.sum(sums_ref[b], axis=0, keepdims=True) * gain_ref[:, span]
                + (rows * cols) * shift_ref[:, span]
            )


def backward_kernel(side, nlow_ref, normed_ref, nhigh_ref, ilow_ref, inv_ref, ihigh_ref,
                    low_ref, x_ref, high_ref, k_ref, weight_ref, centred_ref,
                    grad_ref, taps_grad_ref, pad_ref, gpad_ref, taps_ref, coef_ref):
    step = pl.program_id(0)
    blocks, rows, cols, _ = normed_ref.shape
    channels = blocks * LANES
    reach = side // 2
    parts = (
        (nlow_ref, ilow_ref, 0),
        (normed_ref, inv_ref, reach),
        (nhigh_ref, ihigh_ref, reach + rows),
    )

    @pl.when(step == 0)
    def _():
        clear_edges(pad_ref, cols)
        clear_edges(gpad_ref, cols)
        for n_ref, i_ref, first in parts:
            def one_row(h, carry):
                total = None
                for b in range(blocks):
                    term = n_ref[b, h] * weight_ref[b]
                    total = term if total is None else total + term
                mean = jnp.sum(total, axis=1, keepdims=True) / channels
                coef_ref[first + h] = i_ref[h] * jnp.broadcast_to(mean, (cols, LANES))
                return carry

            lax.fori_loop(0, n_ref.shape[1], one_row, 0)

    fill_taps(taps_ref, k_ref)
    fill_padded(pad_ref, low_ref, x_ref, high_ref)
    for n_ref, i_ref, first in parts:
        for h in range(n_ref.shape[1]):
            gpad_ref[first + h, PAD : PAD + cols, :] = (
                i_ref[h] * centred_ref[step] - n_ref[step, h] * coef_ref[first + h]
            )
    for d in range(side):
        acc = [None] * side
        for w in range(0, cols, 8):
            own = [gpad_ref[reach + h, PAD + w : PAD + w + 8, :] for h in range(rows)]
            for r in range(rows + side - 1):
                x = pad_ref[r, PAD - reach + d + w : PAD - reach + d + w + 8, :]
                for a in range(side):
                    h = r - a
                    if 0 <= h < rows:
                        product = x * own[h]
                        acc[a] = product if acc[a] is None else acc[a] + product
        for a in range(side):
            tap = a * side + d
            taps_grad_ref[tap : tap + 1, :] = jnp.sum(acc[a], axis=0, keepdims=True)
    for start in range(0, cols, TILE):
        acc = convolve(gpad_ref, taps_ref, side, rows, start, True)
        for h in range(rows):
            grad_ref[h, start : start + TILE, :] = acc[h].reshape(TILE, LANES).astype(
                grad_ref.dtype
            )


def entry_barrier(names):
    barrier = pltpu.get_barrier_semaphore()
    count = 0
    for name in names:
        size = lax.axis_size(name)
        me = lax.axis_index(name)
        for j in range(1, size):
            pl.semaphore_signal(
                barrier, inc=1, device_id={name: lax.rem(me + j, size)}, device_id_type=MESH
            )
        count += size - 1
    pl.semaphore_wait(barrier, count)


def exchange(name, source, target, send_sem, recv_sem):
    size = lax.axis_size(name)
    me = lax.axis_index(name)
    copies = []
    for j in range(1, size):
        peer = lax.rem(me + j, size)
        copy = pltpu.make_async_remote_copy(
            src_ref=source(peer),
            dst_ref=target(j),
            send_sem=send_sem.at[j],
            recv_sem=recv_sem.at[j],
            device_id={name: peer},
            device_id_type=MESH,
        )
        copy.start()
        copies.append(copy)
    return copies


def wait_all(copies):
    for copy in copies:
        copy.wait()


def split3(row):
    one = row.astype(jnp.bfloat16)
    rest = row - one.astype(jnp.float32)
    two = rest.astype(jnp.bfloat16)
    three = (rest - two.astype(jnp.float32)).astype(jnp.bfloat16)
    return jnp.concatenate(
        [one, two, three, jnp.zeros((13, row.shape[1]), jnp.bfloat16)], axis=0
    )


def logsum(scores, axis):
    highest = jnp.max(scores, axis=axis, keepdims=True)
    return highest + jnp.log(jnp.sum(jnp.exp(scores - highest), axis=axis, keepdims=True))


def head_kernel(pixel_count, pool_ref, proj_ref, text_ref, gain_ref, scale_ref,
                weight_ref, loss_ref, text_grad_ref,
                pools_ref, txts_ref, imgs_ref, *sems):
    dp, space = lax.axis_size("dp"), lax.axis_size("space")
    me = lax.axis_index("dp")
    entry_barrier(("dp", "space"))
    pool_copies = exchange("space", lambda p: pool_ref, lambda j: pools_ref.at[j], sems[0], sems[1])
    text = text_ref[...]
    text_norm = jnp.sqrt(jnp.sum(text * text, axis=1, keepdims=True))
    unit_txt = text / text_norm
    txts_ref[me] = unit_txt
    txt_copies = exchange(
        "dp", lambda p: txts_ref.at[me], lambda j: txts_ref.at[me], sems[2], sems[3]
    )
    wait_all(pool_copies)
    pools_ref[0] = pool_ref[...]
    mine = lax.axis_index("space")
    pooled = None
    for s in range(space):
        term = pools_ref[lax.rem(mine - s + space, space)]
        pooled = term if pooled is None else pooled + term
    pooled = pooled / pixel_count
    embedded = jnp.sum(
        jnp.dot(split3(pooled), proj_ref[...], preferred_element_type=jnp.float32),
        axis=0, keepdims=True,
    )
    emb_norm = jnp.sqrt(jnp.sum(embedded * embedded, axis=1, keepdims=True))
    unit_img = embedded / emb_norm
    imgs_ref[me] = unit_img
    img_copies = exchange(
        "dp", lambda p: imgs_ref.at[me], lambda j: imgs_ref.at[me], sems[4], sems[5]
    )
    wait_all(txt_copies)
    wait_all(img_copies)
    imgs = jnp.concatenate([imgs_ref[i] for i in range(dp)], axis=0)
    txts = jnp.concatenate([txts_ref[i] for i in range(dp)], axis=0)
    factor = scale_ref[0]
    row_id = lax.broadcasted_iota(jnp.int32, (dp, dp), 0)
    col_id = lax.broadcasted_iota(jnp.int32, (dp, dp), 1)
    scores = jnp.zeros((dp, dp), jnp.float32)
    turned = jnp.zeros((dp, dp), jnp.float32)
    for i in range(dp):
        column = factor * jnp.sum(imgs * txts[i : i + 1], axis=1, keepdims=True)
        scores = jnp.where(col_id == i, column, scores)
        column = factor * jnp.sum(txts * imgs[i : i + 1], axis=1, keepdims=True)
        turned = jnp.where(col_id == i, column, turned)
    identity = (row_id == col_id).astype(jnp.float32)
    row_ls, col_ls = logsum(scores, 1), logsum(scores, 0)
    trow_ls, tcol_ls = logsum(turned, 1), logsum(turned, 0)
    diagonal = jnp.sum(scores * identity, axis=1, keepdims=True)
    tdiagonal = jnp.sum(turned * identity, axis=1, keepdims=True)
    loss = jnp.sum(row_ls - diagonal, axis=0, keepdims=True) + jnp.sum(
        trow_ls - tdiagonal, axis=0, keepdims=True
    )
    loss_ref[...] = loss / (2 * dp)
    grad = 0.5 * (jnp.exp(scores - row_ls) + jnp.exp(scores - col_ls)) - identity
    tgrad = 0.5 * (jnp.exp(turned - trow_ls) + jnp.exp(turned - tcol_ls)) - identity
    own = (col_id == me).astype(jnp.float32)
    own_img = jnp.sum(tgrad * own, axis=1, keepdims=True)
    own_txt = jnp.sum(grad * own, axis=1, keepdims=True)
    unit_img_grad = factor * jnp.sum(own_img * txts, axis=0, keepdims=True)
    unit_txt_grad = factor * jnp.sum(own_txt * imgs, axis=0, keepdims=True)
    text_grad_ref[...] = (
        unit_txt_grad - unit_txt * jnp.sum(unit_txt * unit_txt_grad, axis=1, keepdims=True)
    ) / text_norm
    emb_grad = (
        unit_img_grad - unit_img * jnp.sum(unit_img * unit_img_grad, axis=1, keepdims=True)
    ) / emb_norm
    back = lax.dot_general(
        split3(emb_grad), proj_ref[...], (((1,), (1,)), ((), ())),
        preferred_element_type=jnp.float32,
    )
    weight_ref[...] = jnp.sum(back, axis=0, keepdims=True) * gain_ref[...]


def sum_kernel(part_ref, out_ref, dp_ref, mine_ref, space_ref, *sems):
    dp, space = lax.axis_size("dp"), lax.axis_size("space")
    me_d, me_s = lax.axis_index("dp"), lax.axis_index("space")
    entry_barrier(("dp", "space"))
    wait_all(exchange("dp", lambda p: part_ref.at[p], lambda j: dp_ref.at[j], sems[0], sems[1]))
    total = part_ref[me_d]
    for j in range(1, dp):
        total = total + dp_ref[j]
    mine_ref[...] = total
    wait_all(exchange(
        "space", lambda p: mine_ref.at[p], lambda j: space_ref.at[j], sems[2], sems[3]
    ))
    total = mine_ref[me_s]
    for j in range(1, space):
        total = total + space_ref[j]
    out_ref[me_d, me_s] = total
    wait_all(exchange(
        "space", lambda p: out_ref.at[me_d, me_s], lambda j: out_ref.at[me_d, me_s],
        sems[4], sems[5],
    ))
    wait_all(exchange(
        "dp", lambda p: out_ref.at[me_d], lambda j: out_ref.at[me_d], sems[6], sems[7]
    ))


def neighbours(low_part, high_part):
    count = lax.axis_size("space")
    forward = [(i, i + 1) for i in range(count - 1)]
    backward = [(target, source) for source, target in forward]
    return lax.ppermute(low_part, "space", forward), lax.ppermute(high_part, "space", backward)


def shards(images, dw_kernel, dw_bias, ln_gain, ln_shift, proj, text, logit_scale):
    f32 = jnp.float32
    _, rows, cols, channels = images.shape
    side = dw_kernel.shape[0]
    reach = side // 2
    taps = side * side
    blocks = channels // LANES
    dp, space = lax.axis_size("dp"), lax.axis_size("space")
    pixel_count = rows * space * cols
    vmem = pl.BlockSpec(memory_space=pltpu.VMEM)
    block = images[0]
    low, high = neighbours(block[rows - reach :], block[:reach])
    kernel_rows = dw_kernel.astype(f32).reshape(taps, channels)
    gain = ln_gain.reshape(1, channels)

    def strip(count):
        return pl.BlockSpec((count, cols, LANES), lambda c: (0, 0, c))

    def whole(*shape):
        return pl.BlockSpec(shape, lambda c: (0,) * len(shape))

    lane_row = pl.BlockSpec((1, LANES), lambda c: (0, c))
    tap_rows = pl.BlockSpec((taps, LANES), lambda c: (0, c))
    padded = pltpu.VMEM((rows + 2 * reach, cols + 2 * PAD, LANES), f32)
    normed, inv, pool = pl.pallas_call(
        functools.partial(forward_kernel, side),
        grid=(blocks,),
        in_specs=[strip(reach), strip(rows), strip(reach), tap_rows, lane_row,
                  whole(1, channels), whole(1, channels)],
        out_specs=[whole(blocks, rows, cols, LANES), whole(rows, cols, LANES), whole(1, channels)],
        out_shape=[
            jax.ShapeDtypeStruct((blocks, rows, cols, LANES), f32),
            jax.ShapeDtypeStruct((rows, cols, LANES), f32),
            jax.ShapeDtypeStruct((1, channels), f32),
        ],
        scratch_shapes=[padded, pltpu.VMEM((taps, 8, LANES), f32),
                        pltpu.VMEM((blocks, 8, LANES), f32)],
        compiler_params=pltpu.CompilerParams(vmem_limit_bytes=VMEM_LIMIT),
        name="forward",
    )(low, block, high, kernel_rows, dw_bias.reshape(1, channels), gain,
      ln_shift.reshape(1, channels))
    nlow, nhigh = neighbours(normed[:, rows - reach :], normed[:, :reach])
    ilow, ihigh = neighbours(inv[rows - reach :], inv[:reach])

    embed = proj.shape[1]
    weighted, loss, text_grad = pl.pallas_call(
        functools.partial(head_kernel, pixel_count),
        in_specs=[vmem] * 4 + [pl.BlockSpec(memory_space=pltpu.SMEM)],
        out_specs=[vmem] * 3,
        out_shape=[
            jax.ShapeDtypeStruct((1, channels), f32),
            jax.ShapeDtypeStruct((1, 1), f32),
            jax.ShapeDtypeStruct((1, embed), f32),
        ],
        scratch_shapes=[
            pltpu.VMEM((space, 1, channels), f32),
            pltpu.VMEM((dp, 1, embed), f32),
            pltpu.VMEM((dp, 1, embed), f32),
        ]
        + [pltpu.SemaphoreType.DMA((space,))] * 2
        + [pltpu.SemaphoreType.DMA((dp,))] * 4,
        compiler_params=pltpu.CompilerParams(
            collective_id=0, has_side_effects=True, vmem_limit_bytes=VMEM_LIMIT
        ),
        name="head",
    )(pool, proj, text, gain, logit_scale)
    weight_rows = weighted.reshape(blocks, 1, LANES)
    centred = weight_rows - jnp.mean(weighted)

    grad_images, taps_grad = pl.pallas_call(
        functools.partial(backward_kernel, side),
        grid=(blocks,),
        in_specs=[
            whole(blocks, reach, cols, LANES), whole(blocks, rows, cols, LANES),
            whole(blocks, reach, cols, LANES), whole(reach, cols, LANES),
            whole(rows, cols, LANES), whole(reach, cols, LANES),
            strip(reach), strip(rows), strip(reach), tap_rows,
            whole(blocks, 1, LANES), whole(blocks, 1, LANES),
        ],
        out_specs=[strip(rows), tap_rows],
        out_shape=[
            jax.ShapeDtypeStruct((rows, cols, channels), jnp.bfloat16),
            jax.ShapeDtypeStruct((taps, channels), f32),
        ],
        scratch_shapes=[padded, padded, pltpu.VMEM((taps, 8, LANES), f32),
                        pltpu.VMEM((rows + 2 * reach, cols, LANES), f32)],
        compiler_params=pltpu.CompilerParams(vmem_limit_bytes=VMEM_LIMIT),
        name="backward",
    )(nlow, normed, nhigh, ilow, inv, ihigh, low, block, high, kernel_rows, weight_rows, centred)

    total_rows = taps * blocks
    chunk = -(-total_rows // (dp * space))
    chunk += -chunk % 8
    flat = jnp.pad(taps_grad.reshape(total_rows, LANES),
                   ((0, chunk * dp * space - total_rows), (0, 0)))
    summed = pl.pallas_call(
        sum_kernel,
        in_specs=[vmem],
        out_specs=vmem,
        out_shape=jax.ShapeDtypeStruct((dp, space, chunk, LANES), f32),
        scratch_shapes=[
            pltpu.VMEM((dp, space, chunk, LANES), f32),
            pltpu.VMEM((space, chunk, LANES), f32),
            pltpu.VMEM((space, chunk, LANES), f32),
        ]
        + [pltpu.SemaphoreType.DMA((dp,))] * 2
        + [pltpu.SemaphoreType.DMA((space,))] * 4
        + [pltpu.SemaphoreType.DMA((dp,))] * 2,
        compiler_params=pltpu.CompilerParams(
            collective_id=1, has_side_effects=True, vmem_limit_bytes=VMEM_LIMIT
        ),
        name="kernel_sum",
    )(flat.reshape(dp, space, chunk, LANES))
    kernel_grad = summed.reshape(-1, LANES)[:total_rows].reshape(side, side, channels) / pixel_count
    return loss.reshape(()), grad_images[None], kernel_grad, text_grad


def solution(mesh):
    placed = (P("dp", "space", None, None), P(), P(), P(), P(), P(), P("dp", None), P())
    return jax.shard_map(
        shards,
        mesh=mesh,
        in_specs=placed,
        out_specs=(P(), P("dp", "space", None, None), P(), P("dp", None)),
        check_vma=False,
    )
```

```python
import functools

import jax
import jax.numpy as jnp
from jax import lax
from jax.experimental import pallas as pl
from jax.experimental.pallas import tpu as pltpu
from jax.sharding import PartitionSpec as P

LANES = 128
PAD = 8
TILE = 32
VMEM_LIMIT = 50 * 1024 * 1024
MESH = pl.DeviceIdType.MESH


def fill_taps(taps_ref, rows):
    for i in range(rows.shape[0]):
        taps_ref[i] = jnp.broadcast_to(rows[i : i + 1, :], taps_ref.shape[1:])


def fill_padded(pad_ref, parts, cols):
    first = 0
    for part in parts:
        pad_ref[first : first + part.shape[0], PAD : PAD + cols, :] = part.astype(jnp.float32)
        first += part.shape[0]


def clear_edges(pad_ref, cols):
    rows = pad_ref.shape[0]
    zeros = jnp.zeros((rows, PAD, LANES), jnp.float32)
    pad_ref[:, 0:PAD, :] = zeros
    pad_ref[:, PAD + cols : PAD + cols + PAD, :] = zeros


def convolve(pad_ref, taps_ref, side, rows, start, flip):
    reach = side // 2
    acc = [None] * rows
    for r in range(rows + side - 1):
        for d in range(side):
            first = PAD - reach + d + start
            x = pad_ref[r, first : first + TILE, :].reshape(TILE // 8, 8, LANES)
            for a in range(side):
                h = r - a
                if 0 <= h < rows:
                    tap = (side - 1 - a) * side + side - 1 - d if flip else a * side + d
                    product = x * taps_ref[tap][None]
                    acc[h] = product if acc[h] is None else acc[h] + product
    return acc


def entry_barrier(names):
    barrier = pltpu.get_barrier_semaphore()
    count = 0
    for name in names:
        size = lax.axis_size(name)
        me = lax.axis_index(name)
        for j in range(1, size):
            pl.semaphore_signal(
                barrier, inc=1, device_id={name: lax.rem(me + j, size)}, device_id_type=MESH
            )
        count += size - 1
    pl.semaphore_wait(barrier, count)


def swap(name, source, target, send_sem, recv_sem):
    size = lax.axis_size(name)
    me = lax.axis_index(name)
    copies = []
    for j in range(1, size):
        peer = lax.rem(me + j, size)
        copies.append(pltpu.make_async_remote_copy(
            src_ref=source(peer),
            dst_ref=target(j),
            send_sem=send_sem.at[j],
            recv_sem=recv_sem.at[j],
            device_id={name: peer},
            device_id_type=MESH,
        ))
    return copies


def start_all(copies):
    for copy in copies:
        copy.start()


def exchange(*args):
    copies = swap(*args)
    start_all(copies)
    return copies


def wait_all(copies):
    for copy in copies:
        copy.wait()


def split3(row):
    one = row.astype(jnp.bfloat16)
    rest = row - one.astype(jnp.float32)
    two = rest.astype(jnp.bfloat16)
    three = (rest - two.astype(jnp.float32)).astype(jnp.bfloat16)
    return jnp.concatenate(
        [one, two, three, jnp.zeros((13, row.shape[1]), jnp.bfloat16)], axis=0
    )


def logsum(scores, axis):
    highest = jnp.max(scores, axis=axis, keepdims=True)
    return highest + jnp.log(jnp.sum(jnp.exp(scores - highest), axis=axis, keepdims=True))


def lanes_of(b):
    return pl.ds(pl.multiple_of(b * LANES, LANES), LANES)


def block_kernel(side, pixel_count,
                 image_ref, k_ref, bias_ref, gain_ref, shift_ref, proj_hbm, text_ref, scale_ref,
                 grad_ref, sum_ref, loss_ref, text_grad_ref,
                 low_ref, high_ref, normed_ref, inv_ref, coef_ref, pad_ref, gpad_ref, taps_ref,
                 pool_ref, weight_ref, centred_ref, proj_ref, pools_ref, txts_ref, imgs_ref,
                 part_ref, dp_ref, mine_ref, space_ref,
                 proj_sem, image_sems, wide_sems, *sems):
    rows, cols, channels = image_ref.shape
    blocks = channels // LANES
    reach = side // 2
    dp, space = lax.axis_size("dp"), lax.axis_size("space")
    me, mine = lax.axis_index("dp"), lax.axis_index("space")
    has_low, has_high = mine > 0, mine < space - 1
    share, owned = part_ref.shape[1], part_ref.shape[2] // space

    proj_copy = pltpu.make_async_copy(proj_hbm, proj_ref, proj_sem)
    proj_copy.start()
    entry_barrier(("dp", "space"))

    def to_high(b):
        return pltpu.make_async_remote_copy(
            src_ref=image_ref.at[rows - reach : rows, :, lanes_of(b)], dst_ref=low_ref.at[b],
            send_sem=image_sems.at[0, b], recv_sem=image_sems.at[1, b],
            device_id={"space": mine + 1}, device_id_type=MESH,
        )

    def to_low(b):
        return pltpu.make_async_remote_copy(
            src_ref=image_ref.at[0:reach, :, lanes_of(b)], dst_ref=high_ref.at[b],
            send_sem=image_sems.at[2, b], recv_sem=image_sems.at[3, b],
            device_id={"space": mine - 1}, device_id_type=MESH,
        )

    def send_image(b, carry):
        @pl.when(has_high)
        def _():
            to_high(b).start()

        @pl.when(has_low)
        def _():
            to_low(b).start()

        return carry

    lax.fori_loop(0, blocks, send_image, 0)

    @pl.when(jnp.logical_not(has_low))
    def _():
        low_ref[...] = jnp.zeros_like(low_ref)
        normed_ref[:, 0:reach] = jnp.zeros((blocks, reach, cols, LANES), jnp.float32)
        inv_ref[0:reach] = jnp.zeros((reach, cols, LANES), jnp.float32)

    @pl.when(jnp.logical_not(has_high))
    def _():
        high_ref[...] = jnp.zeros_like(high_ref)
        normed_ref[:, reach + rows :] = jnp.zeros((blocks, reach, cols, LANES), jnp.float32)
        inv_ref[reach + rows :] = jnp.zeros((reach, cols, LANES), jnp.float32)

    text = text_ref[...]
    text_norm = jnp.sqrt(jnp.sum(text * text, axis=1, keepdims=True))
    unit_txt = text / text_norm
    txts_ref[me] = unit_txt
    txt_copies = exchange(
        "dp", lambda p: txts_ref.at[me], lambda j: txts_ref.at[me], sems[2], sems[3]
    )
    clear_edges(pad_ref, cols)
    clear_edges(gpad_ref, cols)

    def forward(b, carry):
        fill_taps(taps_ref, k_ref[:, lanes_of(b)])

        @pl.when(has_low)
        def _():
            to_high(b).wait_recv()

        @pl.when(has_high)
        def _():
            to_low(b).wait_recv()

        fill_padded(pad_ref, (low_ref[b], image_ref[:, :, lanes_of(b)], high_ref[b]), cols)
        bias = bias_ref[:, lanes_of(b)]
        for start in range(0, cols, TILE):
            acc = convolve(pad_ref, taps_ref, side, rows, start, False)
            for h in range(rows):
                normed_ref[b, reach + h, start : start + TILE, :] = (
                    acc[h].reshape(TILE, LANES) + bias
                )
        return carry

    lax.fori_loop(0, blocks, forward, 0)

    weight_ref[...] = jnp.zeros_like(weight_ref)

    def normalize(h, carry):
        r = reach + h
        total = normed_ref[0, r]
        for b in range(1, blocks):
            total = total + normed_ref[b, r]
        mu = jnp.sum(total, axis=1, keepdims=True) / channels
        mu = jnp.broadcast_to(mu, (cols, LANES))
        total = None
        for b in range(blocks):
            centred = normed_ref[b, r] - mu
            total = centred * centred if total is None else total + centred * centred
        spread = jnp.sum(total, axis=1, keepdims=True) / channels
        inv = jnp.broadcast_to(lax.rsqrt(spread + 1e-6), (cols, LANES))
        inv_ref[r] = inv
        for b in range(blocks):
            normed = (normed_ref[b, r] - mu) * inv
            normed_ref[b, r] = normed
            weight_ref[b] += jnp.sum(normed.reshape(cols // 8, 8, LANES), axis=0)
        return carry

    lax.fori_loop(0, rows, normalize, 0)
    for b in range(blocks):
        span = slice(b * LANES, (b + 1) * LANES)
        pool_ref[:, span] = (
            jnp.sum(weight_ref[b], axis=0, keepdims=True) * gain_ref[:, span]
            + (rows * cols) * shift_ref[:, span]
        )
    pool_copies = exchange("space", lambda p: pool_ref, lambda j: pools_ref.at[j], sems[0], sems[1])

    def wide(up):
        copies = []
        for i, ref in enumerate((normed_ref, inv_ref)):
            cut = (lambda a, z: ref.at[:, a:z]) if i == 0 else (lambda a, z: ref.at[a:z])
            source = cut(rows, rows + reach) if up else cut(reach, 2 * reach)
            target = cut(0, reach) if up else cut(rows + reach, rows + 2 * reach)
            copies.append(pltpu.make_async_remote_copy(
                src_ref=source, dst_ref=target,
                send_sem=wide_sems.at[0 if up else 2, i], recv_sem=wide_sems.at[1 if up else 3, i],
                device_id={"space": mine + 1 if up else mine - 1}, device_id_type=MESH,
            ))
        return copies

    @pl.when(has_high)
    def _():
        for copy in wide(True):
            copy.start()

    @pl.when(has_low)
    def _():
        for copy in wide(False):
            copy.start()

    proj_copy.wait()
    wait_all(pool_copies)
    pools_ref[0] = pool_ref[...]
    pooled = None
    for s in range(space):
        term = pools_ref[lax.rem(mine - s + space, space)]
        pooled = term if pooled is None else pooled + term
    pooled = pooled / pixel_count
    embedded = jnp.sum(
        jnp.dot(split3(pooled), proj_ref[...], preferred_element_type=jnp.float32),
        axis=0, keepdims=True,
    )
    emb_norm = jnp.sqrt(jnp.sum(embedded * embedded, axis=1, keepdims=True))
    unit_img = embedded / emb_norm
    imgs_ref[me] = unit_img
    img_copies = exchange(
        "dp", lambda p: imgs_ref.at[me], lambda j: imgs_ref.at[me], sems[4], sems[5]
    )
    wait_all(txt_copies)
    wait_all(img_copies)
    imgs = jnp.concatenate([imgs_ref[i] for i in range(dp)], axis=0)
    txts = jnp.concatenate([txts_ref[i] for i in range(dp)], axis=0)
    factor = scale_ref[0]
    row_id = lax.broadcasted_iota(jnp.int32, (dp, dp), 0)
    col_id = lax.broadcasted_iota(jnp.int32, (dp, dp), 1)
    scores = jnp.zeros((dp, dp), jnp.float32)
    turned = jnp.zeros((dp, dp), jnp.float32)
    for i in range(dp):
        column = factor * jnp.sum(imgs * txts[i : i + 1], axis=1, keepdims=True)
        scores = jnp.where(col_id == i, column, scores)
        column = factor * jnp.sum(txts * imgs[i : i + 1], axis=1, keepdims=True)
        turned = jnp.where(col_id == i, column, turned)
    identity = (row_id == col_id).astype(jnp.float32)
    row_ls, col_ls = logsum(scores, 1), logsum(scores, 0)
    trow_ls, tcol_ls = logsum(turned, 1), logsum(turned, 0)
    diagonal = jnp.sum(scores * identity, axis=1, keepdims=True)
    tdiagonal = jnp.sum(turned * identity, axis=1, keepdims=True)
    loss = jnp.sum(row_ls - diagonal, axis=0, keepdims=True) + jnp.sum(
        trow_ls - tdiagonal, axis=0, keepdims=True
    )
    loss_ref[...] = loss / (2 * dp)
    grad = 0.5 * (jnp.exp(scores - row_ls) + jnp.exp(scores - col_ls)) - identity
    tgrad = 0.5 * (jnp.exp(turned - trow_ls) + jnp.exp(turned - tcol_ls)) - identity
    own = (col_id == me).astype(jnp.float32)
    own_img = jnp.sum(tgrad * own, axis=1, keepdims=True)
    own_txt = jnp.sum(grad * own, axis=1, keepdims=True)
    unit_img_grad = factor * jnp.sum(own_img * txts, axis=0, keepdims=True)
    unit_txt_grad = factor * jnp.sum(own_txt * imgs, axis=0, keepdims=True)
    text_grad_ref[...] = (
        unit_txt_grad - unit_txt * jnp.sum(unit_txt * unit_txt_grad, axis=1, keepdims=True)
    ) / text_norm
    emb_grad = (
        unit_img_grad - unit_img * jnp.sum(unit_img * unit_img_grad, axis=1, keepdims=True)
    ) / emb_norm
    back = lax.dot_general(
        split3(emb_grad), proj_ref[...], (((1,), (1,)), ((), ())),
        preferred_element_type=jnp.float32,
    )
    weighted = jnp.sum(back, axis=0, keepdims=True) * gain_ref[...]
    weight_mean = jnp.sum(weighted, axis=1, keepdims=True) / channels
    for b in range(blocks):
        row = weighted[:, b * LANES : (b + 1) * LANES]
        weight_ref[b] = jnp.broadcast_to(row, (8, LANES))
        centred_ref[b] = jnp.broadcast_to(row - weight_mean, (8, LANES))

    def fill_coef(r, carry):
        total = None
        for b in range(blocks):
            term = normed_ref[b, r].reshape(cols // 8, 8, LANES) * weight_ref[b][None]
            total = term if total is None else total + term
        mean = jnp.sum(total.reshape(cols, LANES), axis=1, keepdims=True) / channels
        coef_ref[r] = inv_ref[r] * jnp.broadcast_to(mean, (cols, LANES))
        return carry

    def fill_grad(b, first, last):
        for r in range(first, last):
            base = (inv_ref[r].reshape(cols // 8, 8, LANES) * centred_ref[b][None]).reshape(
                cols, LANES
            )
            gpad_ref[r, PAD : PAD + cols, :] = base - normed_ref[b, r] * coef_ref[r]

    lax.fori_loop(reach, reach + rows, fill_coef, 0)
    part_ref[...] = jnp.zeros_like(part_ref)

    def kernel_terms(b, carry):
        fill_padded(pad_ref, (low_ref[b], image_ref[:, :, lanes_of(b)], high_ref[b]), cols)
        fill_grad(b, reach, reach + rows)
        for d in range(side):
            acc = [None] * side
            for w in range(0, cols, 8):
                own = [gpad_ref[reach + h, PAD + w : PAD + w + 8, :] for h in range(rows)]
                for r in range(rows + side - 1):
                    x = pad_ref[r, PAD - reach + d + w : PAD - reach + d + w + 8, :]
                    for a in range(side):
                        h = r - a
                        if 0 <= h < rows:
                            product = x * own[h]
                            acc[a] = product if acc[a] is None else acc[a] + product
            for a in range(side):
                part_ref[b // share, b % share, a, d : d + 1, :] = jnp.sum(
                    acc[a], axis=0, keepdims=True
                )
        return carry

    lax.fori_loop(0, blocks, kernel_terms, 0)

    def share_dp():
        return swap("dp", lambda p: part_ref.at[p], lambda j: dp_ref.at[j], sems[6], sems[7])

    def share_space():
        return swap("space", lambda p: mine_ref.at[:, pl.ds(p * owned, owned)],
                    lambda j: space_ref.at[j], sems[8], sems[9])

    def own_piece():
        return sum_ref.at[me, :, pl.ds(mine * owned, owned)]

    def back_space():
        return swap("space", lambda p: own_piece(), lambda j: own_piece(), sems[10], sems[11])

    def back_dp():
        return swap("dp", lambda p: sum_ref.at[me], lambda j: sum_ref.at[me], sems[12], sems[13])

    start_all(share_dp())

    @pl.when(has_high)
    def _():
        for copy in wide(True):
            copy.wait_send()
        for copy in wide(False):
            copy.wait_recv()

    @pl.when(has_low)
    def _():
        for copy in wide(False):
            copy.wait_send()
        for copy in wide(True):
            copy.wait_recv()

    lax.fori_loop(0, reach, fill_coef, 0)
    lax.fori_loop(reach + rows, rows + 2 * reach, fill_coef, 0)

    def input_grad(b, carry):
        @pl.when(b == blocks // 4)
        def _():
            wait_all(share_dp())
            total = part_ref[me]
            for j in range(1, dp):
                total = total + dp_ref[j]
            mine_ref[...] = total
            start_all(share_space())

        @pl.when(b == blocks // 2)
        def _():
            wait_all(share_space())
            total = mine_ref[:, pl.ds(mine * owned, owned)]
            for j in range(1, space):
                total = total + space_ref[j]
            sum_ref[me, :, pl.ds(mine * owned, owned)] = total / pixel_count
            start_all(back_space())

        @pl.when(b == 3 * blocks // 4)
        def _():
            wait_all(back_space())
            start_all(back_dp())

        fill_taps(taps_ref, k_ref[:, lanes_of(b)])
        fill_grad(b, 0, rows + 2 * reach)
        for start in range(0, cols, TILE):
            acc = convolve(gpad_ref, taps_ref, side, rows, start, True)
            for h in range(rows):
                grad_ref[h, start : start + TILE, lanes_of(b)] = (
                    acc[h].reshape(TILE, LANES).astype(grad_ref.dtype)
                )
        return carry

    lax.fori_loop(0, blocks, input_grad, 0)
    wait_all(back_dp())

    def image_sent(b, carry):
        @pl.when(has_high)
        def _():
            to_high(b).wait_send()

        @pl.when(has_low)
        def _():
            to_low(b).wait_send()

        return carry

    lax.fori_loop(0, blocks, image_sent, 0)


def shards(images, dw_kernel, dw_bias, ln_gain, ln_shift, proj, text, logit_scale):
    f32 = jnp.float32
    _, rows, cols, channels = images.shape
    side = dw_kernel.shape[0]
    reach = side // 2
    taps = side * side
    blocks = channels // LANES
    embed = proj.shape[1]
    dp, space = lax.axis_size("dp"), lax.axis_size("space")
    tall = rows + 2 * reach
    share = -(-blocks // dp)
    owned = -(-side // space)
    parts = (dp, share, space * owned, side, LANES)
    vmem = pl.BlockSpec(memory_space=pltpu.VMEM)
    dma = pltpu.SemaphoreType.DMA
    scratch = [
        pltpu.VMEM((blocks, reach, cols, LANES), jnp.bfloat16),
        pltpu.VMEM((blocks, reach, cols, LANES), jnp.bfloat16),
        pltpu.VMEM((blocks, tall, cols, LANES), f32),
        pltpu.VMEM((tall, cols, LANES), f32),
        pltpu.VMEM((tall, cols, LANES), f32),
        pltpu.VMEM((tall, cols + 2 * PAD, LANES), f32),
        pltpu.VMEM((tall, cols + 2 * PAD, LANES), f32),
        pltpu.VMEM((taps, 8, LANES), f32),
        pltpu.VMEM((1, channels), f32),
        pltpu.VMEM((blocks, 8, LANES), f32),
        pltpu.VMEM((blocks, 8, LANES), f32),
        pltpu.VMEM(proj.shape, proj.dtype),
        pltpu.VMEM((space, 1, channels), f32),
        pltpu.VMEM((dp, 1, embed), f32),
        pltpu.VMEM((dp, 1, embed), f32),
        pltpu.VMEM(parts, f32),
        pltpu.VMEM(parts, f32),
        pltpu.VMEM(parts[1:], f32),
        pltpu.VMEM((space, share, owned, side, LANES), f32),
        dma(()),
        dma((4, blocks)),
        dma((4, 2)),
    ]
    for size in (space, dp, dp, dp, space, space, dp):
        scratch += [dma((size,)), dma((size,))]
    grad_images, summed, loss, text_grad = pl.pallas_call(
        functools.partial(block_kernel, side, rows * space * cols),
        in_specs=[vmem] * 5 + [pl.BlockSpec(memory_space=pl.ANY), vmem,
                               pl.BlockSpec(memory_space=pltpu.SMEM)],
        out_specs=[vmem] * 4,
        out_shape=[
            jax.ShapeDtypeStruct((rows, cols, channels), jnp.bfloat16),
            jax.ShapeDtypeStruct(parts, f32),
            jax.ShapeDtypeStruct((1, 1), f32),
            jax.ShapeDtypeStruct((1, embed), f32),
        ],
        scratch_shapes=scratch,
        compiler_params=pltpu.CompilerParams(
            collective_id=0, has_side_effects=True, vmem_limit_bytes=VMEM_LIMIT
        ),
        name="block",
    )(images[0], dw_kernel.astype(f32).reshape(taps, channels), dw_bias.reshape(1, channels),
      ln_gain.reshape(1, channels), ln_shift.reshape(1, channels), proj, text, logit_scale)
    summed = summed.reshape(dp * share, space * owned, side, LANES)[:blocks, :side]
    kernel_grad = jnp.transpose(summed, (1, 2, 0, 3)).reshape(side, side, channels)
    return loss.reshape(()), grad_images[None], kernel_grad, text_grad


def solution(mesh):
    placed = (P("dp", "space", None, None), P(), P(), P(), P(), P(), P("dp", None), P())
    return jax.shard_map(
        shards,
        mesh=mesh,
        in_specs=placed,
        out_specs=(P(), P("dp", "space", None, None), P(), P("dp", None)),
        check_vma=False,
    )
```

```python
import functools

import jax
import jax.numpy as jnp
from jax import lax
from jax.experimental import pallas as pl
from jax.experimental.pallas import tpu as pltpu
from jax.sharding import PartitionSpec as P

LANES = 128
PAD = 8
TILE = 32
VMEM_LIMIT = 63 * 1024 * 1024
MESH = pl.DeviceIdType.MESH


def fill_taps(taps_ref, k_ref, lanes):
    side = k_ref.shape[0]
    for a in range(side):
        rows = k_ref[a, :, lanes].astype(jnp.float32)
        for d in range(side):
            taps_ref[a * side + d] = jnp.broadcast_to(rows[d : d + 1, :], taps_ref.shape[1:])


def fill_padded(pad_ref, parts, cols):
    first = 0
    for part in parts:
        pad_ref[first : first + part.shape[0], PAD : PAD + cols, :] = part.astype(jnp.float32)
        first += part.shape[0]


def clear_edges(pad_ref, cols):
    rows = pad_ref.shape[0]
    zeros = jnp.zeros((rows, PAD, LANES), jnp.float32)
    pad_ref[:, 0:PAD, :] = zeros
    pad_ref[:, PAD + cols : PAD + cols + PAD, :] = zeros


def convolve(pad_ref, taps_ref, side, rows, start, flip):
    reach = side // 2
    acc = [None] * rows
    for r in range(rows + side - 1):
        for d in range(side):
            first = PAD - reach + d + start
            x = pad_ref[r, first : first + TILE, :].reshape(TILE // 8, 8, LANES)
            for a in range(side):
                h = r - a
                if 0 <= h < rows:
                    tap = (side - 1 - a) * side + side - 1 - d if flip else a * side + d
                    product = x * taps_ref[tap][None]
                    acc[h] = product if acc[h] is None else acc[h] + product
    return acc


def entry_barrier(names):
    barrier = pltpu.get_barrier_semaphore()
    count = 0
    for name in names:
        size = lax.axis_size(name)
        me = lax.axis_index(name)
        for j in range(1, size):
            pl.semaphore_signal(
                barrier, inc=1, device_id={name: lax.rem(me + j, size)}, device_id_type=MESH
            )
        count += size - 1
    pl.semaphore_wait(barrier, count)


def swap(name, source, target, send_sem, recv_sem):
    size = lax.axis_size(name)
    me = lax.axis_index(name)
    copies = []
    for j in range(1, size):
        peer = lax.rem(me + j, size)
        copies.append(pltpu.make_async_remote_copy(
            src_ref=source(peer),
            dst_ref=target(j),
            send_sem=send_sem.at[j],
            recv_sem=recv_sem.at[j],
            device_id={name: peer},
            device_id_type=MESH,
        ))
    return copies


def start_all(copies):
    for copy in copies:
        copy.start()


def exchange(*args):
    copies = swap(*args)
    start_all(copies)
    return copies


def wait_all(copies):
    for copy in copies:
        copy.wait()


def split3(row):
    one = row.astype(jnp.bfloat16)
    rest = row - one.astype(jnp.float32)
    two = rest.astype(jnp.bfloat16)
    three = (rest - two.astype(jnp.float32)).astype(jnp.bfloat16)
    return jnp.concatenate(
        [one, two, three, jnp.zeros((13, row.shape[1]), jnp.bfloat16)], axis=0
    )


def logsum(scores, axis):
    highest = jnp.max(scores, axis=axis, keepdims=True)
    return highest + jnp.log(jnp.sum(jnp.exp(scores - highest), axis=axis, keepdims=True))


def lanes_of(b):
    return pl.ds(pl.multiple_of(b * LANES, LANES), LANES)


def block_kernel(side, pixel_count,
                 image_hbm, k_hbm, bias_hbm, gain_hbm, shift_hbm, proj_hbm, text_hbm, scale_ref,
                 grad_ref, sum_ref, loss_ref, text_grad_ref,
                 image_ref, k_ref, bias_ref, gain_ref, shift_ref, text_ref, low_ref, high_ref, normed_ref, inv_ref, coef_ref, pad_ref, gpad_ref, taps_ref,
                 pool_ref, weight_ref, centred_ref, proj_ref, pools_ref, txts_ref, imgs_ref,
                 part_ref, dp_ref, mine_ref, space_ref,
                 local_sems, image_sems, wide_sems, *sems):
    rows, cols, channels = image_hbm.shape
    blocks = channels // LANES
    reach = side // 2
    dp, space = lax.axis_size("dp"), lax.axis_size("space")
    me, mine = lax.axis_index("dp"), lax.axis_index("space")
    has_low, has_high = mine > 0, mine < space - 1
    share, owned = part_ref.shape[1], part_ref.shape[2] // space

    image_copy = pltpu.make_async_copy(image_hbm, image_ref, local_sems.at[0])
    bias_copy = pltpu.make_async_copy(bias_hbm, bias_ref.at[0], local_sems.at[1])
    gain_copy = pltpu.make_async_copy(gain_hbm, gain_ref.at[0], local_sems.at[2])
    shift_copy = pltpu.make_async_copy(shift_hbm, shift_ref.at[0], local_sems.at[3])
    proj_copy = pltpu.make_async_copy(proj_hbm, proj_ref, local_sems.at[4])
    text_copy = pltpu.make_async_copy(text_hbm, text_ref, local_sems.at[5])
    k_copy = pltpu.make_async_copy(k_hbm, k_ref, local_sems.at[6])
    start_all([text_copy, image_copy, k_copy, bias_copy, gain_copy, shift_copy, proj_copy])
    entry_barrier(("dp", "space"))

    def to_high(b):
        return pltpu.make_async_remote_copy(
            src_ref=image_hbm.at[rows - reach : rows, :, lanes_of(b)], dst_ref=low_ref.at[b],
            send_sem=image_sems.at[0, b], recv_sem=image_sems.at[1, b],
            device_id={"space": mine + 1}, device_id_type=MESH,
        )

    def to_low(b):
        return pltpu.make_async_remote_copy(
            src_ref=image_hbm.at[0:reach, :, lanes_of(b)], dst_ref=high_ref.at[b],
            send_sem=image_sems.at[2, b], recv_sem=image_sems.at[3, b],
            device_id={"space": mine - 1}, device_id_type=MESH,
        )

    def send_image(b, carry):
        @pl.when(has_high)
        def _():
            to_high(b).start()

        @pl.when(has_low)
        def _():
            to_low(b).start()

        return carry

    lax.fori_loop(0, blocks, send_image, 0)

    @pl.when(jnp.logical_not(has_low))
    def _():
        low_ref[...] = jnp.zeros_like(low_ref)
        normed_ref[:, 0:reach] = jnp.zeros((blocks, reach, cols, LANES), jnp.float32)
        inv_ref[0:reach] = jnp.zeros((reach, cols, LANES), jnp.float32)

    @pl.when(jnp.logical_not(has_high))
    def _():
        high_ref[...] = jnp.zeros_like(high_ref)
        normed_ref[:, reach + rows :] = jnp.zeros((blocks, reach, cols, LANES), jnp.float32)
        inv_ref[reach + rows :] = jnp.zeros((reach, cols, LANES), jnp.float32)

    text_copy.wait()
    text = text_ref[...]
    text_norm = jnp.sqrt(jnp.sum(text * text, axis=1, keepdims=True))
    unit_txt = text / text_norm
    txts_ref[me] = unit_txt
    txt_copies = exchange(
        "dp", lambda p: txts_ref.at[me], lambda j: txts_ref.at[me], sems[2], sems[3]
    )
    clear_edges(pad_ref, cols)
    clear_edges(gpad_ref, cols)
    wait_all([image_copy, k_copy, bias_copy, gain_copy, shift_copy])

    def forward(b, carry):
        fill_taps(taps_ref, k_ref, lanes_of(b))

        @pl.when(has_low)
        def _():
            to_high(b).wait_recv()

        @pl.when(has_high)
        def _():
            to_low(b).wait_recv()

        fill_padded(pad_ref, (low_ref[b], image_ref[:, :, lanes_of(b)], high_ref[b]), cols)
        bias = bias_ref[:, lanes_of(b)]
        for start in range(0, cols, TILE):
            acc = convolve(pad_ref, taps_ref, side, rows, start, False)
            for h in range(rows):
                normed_ref[b, reach + h, start : start + TILE, :] = (
                    acc[h].reshape(TILE, LANES) + bias
                )
        return carry

    lax.fori_loop(0, blocks, forward, 0)

    weight_ref[...] = jnp.zeros_like(weight_ref)

    def normalize(h, carry):
        r = reach + h
        total = normed_ref[0, r]
        for b in range(1, blocks):
            total = total + normed_ref[b, r]
        mu = jnp.sum(total, axis=1, keepdims=True) / channels
        mu = jnp.broadcast_to(mu, (cols, LANES))
        total = None
        for b in range(blocks):
            centred = normed_ref[b, r] - mu
            total = centred * centred if total is None else total + centred * centred
        spread = jnp.sum(total, axis=1, keepdims=True) / channels
        inv = jnp.broadcast_to(lax.rsqrt(spread + 1e-6), (cols, LANES))
        inv_ref[r] = inv
        for b in range(blocks):
            normed = (normed_ref[b, r] - mu) * inv
            normed_ref[b, r] = normed
            weight_ref[b] += jnp.sum(normed.reshape(cols // 8, 8, LANES), axis=0)
        return carry

    lax.fori_loop(0, rows, normalize, 0)
    for b in range(blocks):
        span = slice(b * LANES, (b + 1) * LANES)
        pool_ref[:, span] = (
            jnp.sum(weight_ref[b], axis=0, keepdims=True) * gain_ref[:, span]
            + (rows * cols) * shift_ref[:, span]
        )
    pool_copies = exchange("space", lambda p: pool_ref, lambda j: pools_ref.at[j], sems[0], sems[1])

    def wide(up):
        copies = []
        for i, ref in enumerate((normed_ref, inv_ref)):
            cut = (lambda a, z: ref.at[:, a:z]) if i == 0 else (lambda a, z: ref.at[a:z])
            source = cut(rows, rows + reach) if up else cut(reach, 2 * reach)
            target = cut(0, reach) if up else cut(rows + reach, rows + 2 * reach)
            copies.append(pltpu.make_async_remote_copy(
                src_ref=source, dst_ref=target,
                send_sem=wide_sems.at[0 if up else 2, i], recv_sem=wide_sems.at[1 if up else 3, i],
                device_id={"space": mine + 1 if up else mine - 1}, device_id_type=MESH,
            ))
        return copies

    proj_copy.wait()
    wait_all(pool_copies)

    @pl.when(has_high)
    def _():
        for copy in wide(True):
            copy.start()

    @pl.when(has_low)
    def _():
        for copy in wide(False):
            copy.start()

    pools_ref[0] = pool_ref[...]
    pooled = None
    for s in range(space):
        term = pools_ref[lax.rem(mine - s + space, space)]
        pooled = term if pooled is None else pooled + term
    pooled = pooled / pixel_count
    embedded = jnp.sum(
        jnp.dot(split3(pooled), proj_ref[...], preferred_element_type=jnp.float32),
        axis=0, keepdims=True,
    )
    emb_norm = jnp.sqrt(jnp.sum(embedded * embedded, axis=1, keepdims=True))
    unit_img = embedded / emb_norm
    imgs_ref[me] = unit_img
    img_copies = exchange(
        "dp", lambda p: imgs_ref.at[me], lambda j: imgs_ref.at[me], sems[4], sems[5]
    )
    wait_all(txt_copies)
    wait_all(img_copies)
    imgs = jnp.concatenate([imgs_ref[i] for i in range(dp)], axis=0)
    txts = jnp.concatenate([txts_ref[i] for i in range(dp)], axis=0)
    factor = scale_ref[0]
    row_id = lax.broadcasted_iota(jnp.int32, (dp, dp), 0)
    col_id = lax.broadcasted_iota(jnp.int32, (dp, dp), 1)
    scores = jnp.zeros((dp, dp), jnp.float32)
    turned = jnp.zeros((dp, dp), jnp.float32)
    for i in range(dp):
        column = factor * jnp.sum(imgs * txts[i : i + 1], axis=1, keepdims=True)
        scores = jnp.where(col_id == i, column, scores)
        column = factor * jnp.sum(txts * imgs[i : i + 1], axis=1, keepdims=True)
        turned = jnp.where(col_id == i, column, turned)
    identity = (row_id == col_id).astype(jnp.float32)
    row_ls, col_ls = logsum(scores, 1), logsum(scores, 0)
    trow_ls, tcol_ls = logsum(turned, 1), logsum(turned, 0)
    diagonal = jnp.sum(scores * identity, axis=1, keepdims=True)
    tdiagonal = jnp.sum(turned * identity, axis=1, keepdims=True)
    loss = jnp.sum(row_ls - diagonal, axis=0, keepdims=True) + jnp.sum(
        trow_ls - tdiagonal, axis=0, keepdims=True
    )
    loss_ref[...] = loss / (2 * dp)
    grad = 0.5 * (jnp.exp(scores - row_ls) + jnp.exp(scores - col_ls)) - identity
    tgrad = 0.5 * (jnp.exp(turned - trow_ls) + jnp.exp(turned - tcol_ls)) - identity
    own = (col_id == me).astype(jnp.float32)
    own_img = jnp.sum(tgrad * own, axis=1, keepdims=True)
    own_txt = jnp.sum(grad * own, axis=1, keepdims=True)
    unit_img_grad = factor * jnp.sum(own_img * txts, axis=0, keepdims=True)
    unit_txt_grad = factor * jnp.sum(own_txt * imgs, axis=0, keepdims=True)
    text_grad_ref[...] = (
        unit_txt_grad - unit_txt * jnp.sum(unit_txt * unit_txt_grad, axis=1, keepdims=True)
    ) / text_norm
    emb_grad = (
        unit_img_grad - unit_img * jnp.sum(unit_img * unit_img_grad, axis=1, keepdims=True)
    ) / emb_norm
    back = lax.dot_general(
        split3(emb_grad), proj_ref[...], (((1,), (1,)), ((), ())),
        preferred_element_type=jnp.float32,
    )
    weighted = jnp.sum(back, axis=0, keepdims=True) * gain_ref[...]
    weight_mean = jnp.sum(weighted, axis=1, keepdims=True) / channels
    for b in range(blocks):
        row = weighted[:, b * LANES : (b + 1) * LANES]
        weight_ref[b] = jnp.broadcast_to(row, (8, LANES))
        centred_ref[b] = jnp.broadcast_to(row - weight_mean, (8, LANES))

    def fill_coef(r, carry):
        total = None
        for b in range(blocks):
            term = normed_ref[b, r].reshape(cols // 8, 8, LANES) * weight_ref[b][None]
            total = term if total is None else total + term
        mean = jnp.sum(total.reshape(cols, LANES), axis=1, keepdims=True) / channels
        coef_ref[r] = inv_ref[r] * jnp.broadcast_to(mean, (cols, LANES))
        return carry

    def fill_grad(b, first, last):
        for r in range(first, last):
            base = (inv_ref[r].reshape(cols // 8, 8, LANES) * centred_ref[b][None]).reshape(
                cols, LANES
            )
            gpad_ref[r, PAD : PAD + cols, :] = base - normed_ref[b, r] * coef_ref[r]

    lax.fori_loop(reach, reach + rows, fill_coef, 0)
    part_ref[...] = jnp.zeros_like(part_ref)

    def kernel_terms(b, carry):
        fill_padded(pad_ref, (low_ref[b], image_ref[:, :, lanes_of(b)], high_ref[b]), cols)
        fill_grad(b, reach, reach + rows)
        for d in range(side):
            acc = [None] * side
            for w in range(0, cols, 8):
                own = [gpad_ref[reach + h, PAD + w : PAD + w + 8, :] for h in range(rows)]
                for r in range(rows + side - 1):
                    x = pad_ref[r, PAD - reach + d + w : PAD - reach + d + w + 8, :]
                    for a in range(side):
                        h = r - a
                        if 0 <= h < rows:
                            product = x * own[h]
                            acc[a] = product if acc[a] is None else acc[a] + product
            for a in range(side):
                part_ref[b // share, b % share, a, d : d + 1, :] = jnp.sum(
                    acc[a], axis=0, keepdims=True
                )
        return carry

    lax.fori_loop(0, blocks, kernel_terms, 0)

    def share_dp():
        return swap("dp", lambda p: part_ref.at[p], lambda j: dp_ref.at[j], sems[6], sems[7])

    def share_space():
        return swap("space", lambda p: mine_ref.at[:, pl.ds(p * owned, owned)],
                    lambda j: space_ref.at[j], sems[8], sems[9])

    def own_piece():
        return sum_ref.at[me, :, pl.ds(mine * owned, owned)]

    def back_space():
        return swap("space", lambda p: own_piece(), lambda j: own_piece(), sems[10], sems[11])

    def back_dp():
        return swap("dp", lambda p: sum_ref.at[me], lambda j: sum_ref.at[me], sems[12], sems[13])

    start_all(share_dp())

    @pl.when(has_high)
    def _():
        for copy in wide(True):
            copy.wait_send()
        for copy in wide(False):
            copy.wait_recv()

    @pl.when(has_low)
    def _():
        for copy in wide(False):
            copy.wait_send()
        for copy in wide(True):
            copy.wait_recv()

    lax.fori_loop(0, reach, fill_coef, 0)
    lax.fori_loop(reach + rows, rows + 2 * reach, fill_coef, 0)

    def input_grad(b, carry):
        @pl.when(b == blocks // 4)
        def _():
            wait_all(share_dp())
            total = part_ref[me]
            for j in range(1, dp):
                total = total + dp_ref[j]
            mine_ref[...] = total
            start_all(share_space())

        @pl.when(b == blocks // 2)
        def _():
            wait_all(share_space())
            total = mine_ref[:, pl.ds(mine * owned, owned)]
            for j in range(1, space):
                total = total + space_ref[j]
            sum_ref[me, :, pl.ds(mine * owned, owned)] = total / pixel_count
            start_all(back_space())

        @pl.when(b == 3 * blocks // 4)
        def _():
            wait_all(back_space())
            start_all(back_dp())

        fill_taps(taps_ref, k_ref, lanes_of(b))
        fill_grad(b, 0, rows + 2 * reach)
        for start in range(0, cols, TILE):
            acc = convolve(gpad_ref, taps_ref, side, rows, start, True)
            for h in range(rows):
                grad_ref[h, start : start + TILE, lanes_of(b)] = (
                    acc[h].reshape(TILE, LANES).astype(grad_ref.dtype)
                )
        return carry

    lax.fori_loop(0, blocks, input_grad, 0)
    wait_all(back_dp())

    def image_sent(b, carry):
        @pl.when(has_high)
        def _():
            to_high(b).wait_send()

        @pl.when(has_low)
        def _():
            to_low(b).wait_send()

        return carry

    lax.fori_loop(0, blocks, image_sent, 0)


def shards(images, dw_kernel, dw_bias, ln_gain, ln_shift, proj, text, logit_scale):
    f32 = jnp.float32
    _, rows, cols, channels = images.shape
    side = dw_kernel.shape[0]
    reach = side // 2
    taps = side * side
    blocks = channels // LANES
    embed = proj.shape[1]
    dp, space = lax.axis_size("dp"), lax.axis_size("space")
    tall = rows + 2 * reach
    share = -(-blocks // dp)
    owned = -(-side // space)
    parts = (dp, share, space * owned, side, LANES)
    vmem = pl.BlockSpec(memory_space=pltpu.VMEM)
    hbm = pl.BlockSpec(memory_space=pltpu.HBM)
    dma = pltpu.SemaphoreType.DMA
    scratch = [
        pltpu.VMEM((rows, cols, channels), jnp.bfloat16),
        pltpu.VMEM(dw_kernel.shape, dw_kernel.dtype),
        pltpu.VMEM((1, channels), f32),
        pltpu.VMEM((1, channels), f32),
        pltpu.VMEM((1, channels), f32),
        pltpu.VMEM((1, embed), f32),
        pltpu.VMEM((blocks, reach, cols, LANES), jnp.bfloat16),
        pltpu.VMEM((blocks, reach, cols, LANES), jnp.bfloat16),
        pltpu.VMEM((blocks, tall, cols, LANES), f32),
        pltpu.VMEM((tall, cols, LANES), f32),
        pltpu.VMEM((tall, cols, LANES), f32),
        pltpu.VMEM((tall, cols + 2 * PAD, LANES), f32),
        pltpu.VMEM((tall, cols + 2 * PAD, LANES), f32),
        pltpu.VMEM((taps, 8, LANES), f32),
        pltpu.VMEM((1, channels), f32),
        pltpu.VMEM((blocks, 8, LANES), f32),
        pltpu.VMEM((blocks, 8, LANES), f32),
        pltpu.VMEM(proj.shape, proj.dtype),
        pltpu.VMEM((space, 1, channels), f32),
        pltpu.VMEM((dp, 1, embed), f32),
        pltpu.VMEM((dp, 1, embed), f32),
        pltpu.VMEM(parts, f32),
        pltpu.VMEM(parts, f32),
        pltpu.VMEM(parts[1:], f32),
        pltpu.VMEM((space, share, owned, side, LANES), f32),
        dma((7,)),
        dma((4, blocks)),
        dma((4, 2)),
    ]
    for size in (space, dp, dp, dp, space, space, dp):
        scratch += [dma((size,)), dma((size,))]
    grad_images, summed, loss, text_grad = pl.pallas_call(
        functools.partial(block_kernel, side, rows * space * cols),
        in_specs=[hbm] * 7 + [
                               pl.BlockSpec(memory_space=pltpu.SMEM)],
        out_specs=[vmem] * 4,
        out_shape=[
            jax.ShapeDtypeStruct((rows, cols, channels), jnp.bfloat16),
            jax.ShapeDtypeStruct(parts, f32),
            jax.ShapeDtypeStruct((1, 1), f32),
            jax.ShapeDtypeStruct((1, embed), f32),
        ],
        scratch_shapes=scratch,
        compiler_params=pltpu.CompilerParams(
            collective_id=0, has_side_effects=True, vmem_limit_bytes=VMEM_LIMIT
        ),
        name="block",
    )(images[0], dw_kernel, dw_bias, ln_gain, ln_shift, proj, text, logit_scale)
    summed = summed.reshape(dp * share, space * owned, side, LANES)[:blocks, :side]
    kernel_grad = jnp.transpose(summed, (1, 2, 0, 3)).reshape(side, side, channels)
    return loss.reshape(()), grad_images[None], kernel_grad, text_grad


def solution(mesh):
    placed = (P("dp", "space", None, None), P(), P(), P(), P(), P(), P("dp", None), P())
    return jax.shard_map(
        shards,
        mesh=mesh,
        in_specs=placed,
        out_specs=(P(), P("dp", "space", None, None), P(), P("dp", None)),
        check_vma=False,
    )
```

```python
import functools

import jax
import jax.numpy as jnp
from jax import lax
from jax.experimental import pallas as pl
from jax.experimental.pallas import tpu as pltpu
from jax.sharding import PartitionSpec as P

LANES = 128
PAD = 8
TILE = 32
VMEM_LIMIT = 63 * 1024 * 1024
MESH = pl.DeviceIdType.MESH


def fill_taps(taps_ref, k_ref, lanes):
    side = k_ref.shape[0]
    for a in range(side):
        rows = k_ref[a, :, lanes].astype(jnp.float32)
        for d in range(side):
            taps_ref[a * side + d] = jnp.broadcast_to(rows[d : d + 1, :], taps_ref.shape[1:])


def fill_padded(pad_ref, parts, cols):
    first = 0
    for part in parts:
        pad_ref[first : first + part.shape[0], PAD : PAD + cols, :] = part.astype(jnp.float32)
        first += part.shape[0]


def clear_edges(pad_ref, cols):
    rows = pad_ref.shape[0]
    zeros = jnp.zeros((rows, PAD, LANES), jnp.float32)
    pad_ref[:, 0:PAD, :] = zeros
    pad_ref[:, PAD + cols : PAD + cols + PAD, :] = zeros


def convolve(pad_ref, taps_ref, side, rows, start, flip):
    reach = side // 2
    acc = [None] * rows
    for r in range(rows + side - 1):
        for d in range(side):
            first = PAD - reach + d + start
            x = pad_ref[r, first : first + TILE, :].reshape(TILE // 8, 8, LANES)
            for a in range(side):
                h = r - a
                if 0 <= h < rows:
                    tap = (side - 1 - a) * side + side - 1 - d if flip else a * side + d
                    product = x * taps_ref[tap][None]
                    acc[h] = product if acc[h] is None else acc[h] + product
    return acc


def entry_barrier(names):
    barrier = pltpu.get_barrier_semaphore()
    count = 0
    for name in names:
        size = lax.axis_size(name)
        me = lax.axis_index(name)
        for j in range(1, size):
            pl.semaphore_signal(
                barrier, inc=1, device_id={name: lax.rem(me + j, size)}, device_id_type=MESH
            )
        count += size - 1
    pl.semaphore_wait(barrier, count)


def swap(name, source, target, send_sem, recv_sem):
    size = lax.axis_size(name)
    me = lax.axis_index(name)
    copies = []
    for j in range(1, size):
        peer = lax.rem(me + j, size)
        copies.append(pltpu.make_async_remote_copy(
            src_ref=source(peer),
            dst_ref=target(j),
            send_sem=send_sem.at[j],
            recv_sem=recv_sem.at[j],
            device_id={name: peer},
            device_id_type=MESH,
        ))
    return copies


def start_all(copies):
    for copy in copies:
        copy.start()


def exchange(*args):
    copies = swap(*args)
    start_all(copies)
    return copies


def wait_all(copies):
    for copy in copies:
        copy.wait()


def split3(row):
    one = row.astype(jnp.bfloat16)
    rest = row - one.astype(jnp.float32)
    two = rest.astype(jnp.bfloat16)
    three = (rest - two.astype(jnp.float32)).astype(jnp.bfloat16)
    return jnp.concatenate(
        [one, two, three, jnp.zeros((13, row.shape[1]), jnp.bfloat16)], axis=0
    )


def logsum(scores, axis):
    highest = jnp.max(scores, axis=axis, keepdims=True)
    return highest + jnp.log(jnp.sum(jnp.exp(scores - highest), axis=axis, keepdims=True))


def lanes_of(b):
    return pl.ds(pl.multiple_of(b * LANES, LANES), LANES)


def block_kernel(side, pixel_count,
                 image_hbm, k_hbm, bias_hbm, gain_hbm, shift_hbm, proj_hbm, text_hbm, scale_ref,
                 grad_ref, sum_ref, loss_ref, text_grad_ref,
                 image_ref, k_ref, bias_ref, gain_ref, shift_ref, text_ref, low_ref, high_ref, normed_ref, inv_ref, coef_ref, pad_ref, gpad_ref, taps_ref,
                 pool_ref, weight_ref, centred_ref, proj_ref, turned_ref, pools_ref, txts_ref, imgs_ref,
                 part_ref, dp_ref, mine_ref, space_ref,
                 local_sems, image_sems, wide_sems, *sems):
    rows, cols, channels = image_hbm.shape
    blocks = channels // LANES
    reach = side // 2
    dp, space = lax.axis_size("dp"), lax.axis_size("space")
    me, mine = lax.axis_index("dp"), lax.axis_index("space")
    has_low, has_high = mine > 0, mine < space - 1
    share, owned = part_ref.shape[1], part_ref.shape[2] // space

    image_copy = pltpu.make_async_copy(image_hbm, image_ref, local_sems.at[0])
    bias_copy = pltpu.make_async_copy(bias_hbm, bias_ref.at[0], local_sems.at[1])
    gain_copy = pltpu.make_async_copy(gain_hbm, gain_ref.at[0], local_sems.at[2])
    shift_copy = pltpu.make_async_copy(shift_hbm, shift_ref.at[0], local_sems.at[3])
    proj_copy = pltpu.make_async_copy(proj_hbm, proj_ref, local_sems.at[4])
    text_copy = pltpu.make_async_copy(text_hbm, text_ref, local_sems.at[5])
    k_copy = pltpu.make_async_copy(k_hbm, k_ref, local_sems.at[6])
    start_all([text_copy, image_copy, k_copy, bias_copy, gain_copy, shift_copy, proj_copy])
    entry_barrier(("dp", "space"))

    def to_high(b):
        return pltpu.make_async_remote_copy(
            src_ref=image_hbm.at[rows - reach : rows, :, lanes_of(b)], dst_ref=low_ref.at[b],
            send_sem=image_sems.at[0, b], recv_sem=image_sems.at[1, b],
            device_id={"space": mine + 1}, device_id_type=MESH,
        )

    def to_low(b):
        return pltpu.make_async_remote_copy(
            src_ref=image_hbm.at[0:reach, :, lanes_of(b)], dst_ref=high_ref.at[b],
            send_sem=image_sems.at[2, b], recv_sem=image_sems.at[3, b],
            device_id={"space": mine - 1}, device_id_type=MESH,
        )

    def send_image(b, carry):
        @pl.when(has_high)
        def _():
            to_high(b).start()

        @pl.when(has_low)
        def _():
            to_low(b).start()

        return carry

    lax.fori_loop(0, blocks, send_image, 0)

    @pl.when(jnp.logical_not(has_low))
    def _():
        low_ref[...] = jnp.zeros_like(low_ref)
        normed_ref[:, 0:reach] = jnp.zeros((blocks, reach, cols, LANES), jnp.float32)
        inv_ref[0:reach] = jnp.zeros((reach, cols, LANES), jnp.float32)

    @pl.when(jnp.logical_not(has_high))
    def _():
        high_ref[...] = jnp.zeros_like(high_ref)
        normed_ref[:, reach + rows :] = jnp.zeros((blocks, reach, cols, LANES), jnp.float32)
        inv_ref[reach + rows :] = jnp.zeros((reach, cols, LANES), jnp.float32)

    text_copy.wait()
    text = text_ref[...]
    text_norm = jnp.sqrt(jnp.sum(text * text, axis=1, keepdims=True))
    unit_txt = text / text_norm
    txts_ref[me] = unit_txt
    txt_copies = exchange(
        "dp", lambda p: txts_ref.at[me], lambda j: txts_ref.at[me], sems[2], sems[3]
    )
    clear_edges(pad_ref, cols)
    clear_edges(gpad_ref, cols)
    proj_copy.wait()
    for b in range(blocks):
        span = slice(b * LANES, (b + 1) * LANES)
        turned_ref[:, span] = proj_ref[span, :].T
    wait_all([image_copy, k_copy, bias_copy, gain_copy, shift_copy])

    def forward(b, carry):
        fill_taps(taps_ref, k_ref, lanes_of(b))

        @pl.when(has_low)
        def _():
            to_high(b).wait_recv()

        @pl.when(has_high)
        def _():
            to_low(b).wait_recv()

        fill_padded(pad_ref, (low_ref[b], image_ref[:, :, lanes_of(b)], high_ref[b]), cols)
        bias = bias_ref[:, lanes_of(b)]
        for start in range(0, cols, TILE):
            acc = convolve(pad_ref, taps_ref, side, rows, start, False)
            for h in range(rows):
                normed_ref[b, reach + h, start : start + TILE, :] = (
                    acc[h].reshape(TILE, LANES) + bias
                )
        return carry

    lax.fori_loop(0, blocks, forward, 0)

    weight_ref[...] = jnp.zeros_like(weight_ref)

    def normalize(h, carry):
        r = reach + h
        total = normed_ref[0, r]
        for b in range(1, blocks):
            total = total + normed_ref[b, r]
        mu = jnp.sum(total, axis=1, keepdims=True) / channels
        mu = jnp.broadcast_to(mu, (cols, LANES))
        total = None
        for b in range(blocks):
            centred = normed_ref[b, r] - mu
            total = centred * centred if total is None else total + centred * centred
        spread = jnp.sum(total, axis=1, keepdims=True) / channels
        inv = jnp.broadcast_to(lax.rsqrt(spread + 1e-6), (cols, LANES))
        inv_ref[r] = inv
        for b in range(blocks):
            normed = (normed_ref[b, r] - mu) * inv
            normed_ref[b, r] = normed
            weight_ref[b] += jnp.sum(normed.reshape(cols // 8, 8, LANES), axis=0)
        return carry

    lax.fori_loop(0, rows, normalize, 0)
    for b in range(blocks):
        span = slice(b * LANES, (b + 1) * LANES)
        pool_ref[:, span] = (
            jnp.sum(weight_ref[b], axis=0, keepdims=True) * gain_ref[:, span]
            + (rows * cols) * shift_ref[:, span]
        )
    pool_copies = exchange("space", lambda p: pool_ref, lambda j: pools_ref.at[j], sems[0], sems[1])

    def wide(up):
        copies = []
        for i, ref in enumerate((normed_ref, inv_ref)):
            cut = (lambda a, z: ref.at[:, a:z]) if i == 0 else (lambda a, z: ref.at[a:z])
            source = cut(rows, rows + reach) if up else cut(reach, 2 * reach)
            target = cut(0, reach) if up else cut(rows + reach, rows + 2 * reach)
            copies.append(pltpu.make_async_remote_copy(
                src_ref=source, dst_ref=target,
                send_sem=wide_sems.at[0 if up else 2, i], recv_sem=wide_sems.at[1 if up else 3, i],
                device_id={"space": mine + 1 if up else mine - 1}, device_id_type=MESH,
            ))
        return copies

    wait_all(pool_copies)

    @pl.when(has_high)
    def _():
        for copy in wide(True):
            copy.start()

    @pl.when(has_low)
    def _():
        for copy in wide(False):
            copy.start()

    pools_ref[0] = pool_ref[...]
    pooled = None
    for s in range(space):
        term = pools_ref[lax.rem(mine - s + space, space)]
        pooled = term if pooled is None else pooled + term
    pooled = pooled / pixel_count
    embedded = jnp.sum(
        jnp.dot(split3(pooled), proj_ref[...], preferred_element_type=jnp.float32),
        axis=0, keepdims=True,
    )
    emb_norm = jnp.sqrt(jnp.sum(embedded * embedded, axis=1, keepdims=True))
    unit_img = embedded / emb_norm
    imgs_ref[me] = unit_img
    img_copies = exchange(
        "dp", lambda p: imgs_ref.at[me], lambda j: imgs_ref.at[me], sems[4], sems[5]
    )
    wait_all(txt_copies)
    wait_all(img_copies)
    imgs = jnp.concatenate([imgs_ref[i] for i in range(dp)], axis=0)
    txts = jnp.concatenate([txts_ref[i] for i in range(dp)], axis=0)
    factor = scale_ref[0]
    row_id = lax.broadcasted_iota(jnp.int32, (dp, dp), 0)
    col_id = lax.broadcasted_iota(jnp.int32, (dp, dp), 1)
    scores = jnp.zeros((dp, dp), jnp.float32)
    turned = jnp.zeros((dp, dp), jnp.float32)
    for i in range(dp):
        column = factor * jnp.sum(imgs * txts[i : i + 1], axis=1, keepdims=True)
        scores = jnp.where(col_id == i, column, scores)
        column = factor * jnp.sum(txts * imgs[i : i + 1], axis=1, keepdims=True)
        turned = jnp.where(col_id == i, column, turned)
    identity = (row_id == col_id).astype(jnp.float32)
    row_ls, col_ls = logsum(scores, 1), logsum(scores, 0)
    trow_ls, tcol_ls = logsum(turned, 1), logsum(turned, 0)
    diagonal = jnp.sum(scores * identity, axis=1, keepdims=True)
    tdiagonal = jnp.sum(turned * identity, axis=1, keepdims=True)
    loss = jnp.sum(row_ls - diagonal, axis=0, keepdims=True) + jnp.sum(
        trow_ls - tdiagonal, axis=0, keepdims=True
    )
    loss_ref[...] = loss / (2 * dp)
    grad = 0.5 * (jnp.exp(scores - row_ls) + jnp.exp(scores - col_ls)) - identity
    tgrad = 0.5 * (jnp.exp(turned - trow_ls) + jnp.exp(turned - tcol_ls)) - identity
    own = (col_id == me).astype(jnp.float32)
    own_img = jnp.sum(tgrad * own, axis=1, keepdims=True)
    own_txt = jnp.sum(grad * own, axis=1, keepdims=True)
    unit_img_grad = factor * jnp.sum(own_img * txts, axis=0, keepdims=True)
    unit_txt_grad = factor * jnp.sum(own_txt * imgs, axis=0, keepdims=True)
    text_grad_ref[...] = (
        unit_txt_grad - unit_txt * jnp.sum(unit_txt * unit_txt_grad, axis=1, keepdims=True)
    ) / text_norm
    emb_grad = (
        unit_img_grad - unit_img * jnp.sum(unit_img * unit_img_grad, axis=1, keepdims=True)
    ) / emb_norm
    back = jnp.dot(split3(emb_grad), turned_ref[...], preferred_element_type=jnp.float32)
    weighted = jnp.sum(back, axis=0, keepdims=True) * gain_ref[...]
    weight_mean = jnp.sum(weighted, axis=1, keepdims=True) / channels
    for b in range(blocks):
        row = weighted[:, b * LANES : (b + 1) * LANES]
        weight_ref[b] = jnp.broadcast_to(row, (8, LANES))
        centred_ref[b] = jnp.broadcast_to(row - weight_mean, (8, LANES))

    def fill_coef(r, carry):
        total = None
        for b in range(blocks):
            term = normed_ref[b, r].reshape(cols // 8, 8, LANES) * weight_ref[b][None]
            total = term if total is None else total + term
        mean = jnp.sum(total.reshape(cols, LANES), axis=1, keepdims=True) / channels
        coef_ref[r] = inv_ref[r] * jnp.broadcast_to(mean, (cols, LANES))
        return carry

    def fill_grad(b, first, last):
        for r in range(first, last):
            base = (inv_ref[r].reshape(cols // 8, 8, LANES) * centred_ref[b][None]).reshape(
                cols, LANES
            )
            gpad_ref[r, PAD : PAD + cols, :] = base - normed_ref[b, r] * coef_ref[r]

    lax.fori_loop(reach, reach + rows, fill_coef, 0)
    part_ref[...] = jnp.zeros_like(part_ref)

    def piece(owner, k, j):
        return pltpu.make_async_remote_copy(
            src_ref=part_ref.at[owner, k], dst_ref=dp_ref.at[j, k],
            send_sem=sems[6].at[j, k], recv_sem=sems[7].at[j, k],
            device_id={"dp": owner}, device_id_type=MESH,
        )

    def to_owner(b):
        return piece(b // share, b % share, lax.rem(b // share - me + dp, dp))

    def kernel_terms(b, carry):
        fill_padded(pad_ref, (low_ref[b], image_ref[:, :, lanes_of(b)], high_ref[b]), cols)
        fill_grad(b, reach, reach + rows)
        for d in range(side):
            acc = [None] * side
            for w in range(0, cols, 8):
                own = [gpad_ref[reach + h, PAD + w : PAD + w + 8, :] for h in range(rows)]
                for r in range(rows + side - 1):
                    x = pad_ref[r, PAD - reach + d + w : PAD - reach + d + w + 8, :]
                    for a in range(side):
                        h = r - a
                        if 0 <= h < rows:
                            product = x * own[h]
                            acc[a] = product if acc[a] is None else acc[a] + product
            for a in range(side):
                part_ref[b // share, b % share, a, d : d + 1, :] = jnp.sum(
                    acc[a], axis=0, keepdims=True
                )

        @pl.when(b // share != me)
        def _():
            to_owner(b).start()

        return carry

    lax.fori_loop(0, blocks, kernel_terms, 0)

    def share_space():
        return swap("space", lambda p: mine_ref.at[:, pl.ds(p * owned, owned)],
                    lambda j: space_ref.at[j], sems[8], sems[9])

    def own_piece():
        return sum_ref.at[me, :, pl.ds(mine * owned, owned)]

    def back_space():
        return swap("space", lambda p: own_piece(), lambda j: own_piece(), sems[10], sems[11])

    def back_dp():
        return swap("dp", lambda p: sum_ref.at[me], lambda j: sum_ref.at[me], sems[12], sems[13])

    @pl.when(has_high)
    def _():
        for copy in wide(True):
            copy.wait_send()
        for copy in wide(False):
            copy.wait_recv()

    @pl.when(has_low)
    def _():
        for copy in wide(False):
            copy.wait_send()
        for copy in wide(True):
            copy.wait_recv()

    lax.fori_loop(0, reach, fill_coef, 0)
    lax.fori_loop(reach + rows, rows + 2 * reach, fill_coef, 0)

    def input_grad(b, carry):
        @pl.when(b == 1)
        def _():
            for j in range(1, dp):
                for k in range(share):
                    @pl.when(me * share + k < blocks)
                    def _():
                        piece(lax.rem(me + j, dp), k, j).wait_recv()
            total = part_ref[me]
            for j in range(1, dp):
                total = total + dp_ref[j]
            mine_ref[...] = total
            start_all(share_space())

        @pl.when(b == blocks // 3)
        def _():
            wait_all(share_space())
            total = mine_ref[:, pl.ds(mine * owned, owned)]
            for j in range(1, space):
                total = total + space_ref[j]
            sum_ref[me, :, pl.ds(mine * owned, owned)] = total / pixel_count
            start_all(back_space())

        @pl.when(b == 7 * blocks // 12)
        def _():
            wait_all(back_space())
            start_all(back_dp())

        fill_taps(taps_ref, k_ref, lanes_of(b))
        fill_grad(b, 0, rows + 2 * reach)
        for start in range(0, cols, TILE):
            acc = convolve(gpad_ref, taps_ref, side, rows, start, True)
            for h in range(rows):
                grad_ref[h, start : start + TILE, lanes_of(b)] = (
                    acc[h].reshape(TILE, LANES).astype(grad_ref.dtype)
                )
        return carry

    lax.fori_loop(0, blocks, input_grad, 0)
    wait_all(back_dp())

    def image_sent(b, carry):
        @pl.when(b // share != me)
        def _():
            to_owner(b).wait_send()

        @pl.when(has_high)
        def _():
            to_high(b).wait_send()

        @pl.when(has_low)
        def _():
            to_low(b).wait_send()

        return carry

    lax.fori_loop(0, blocks, image_sent, 0)


def shards(images, dw_kernel, dw_bias, ln_gain, ln_shift, proj, text, logit_scale):
    f32 = jnp.float32
    _, rows, cols, channels = images.shape
    side = dw_kernel.shape[0]
    reach = side // 2
    taps = side * side
    blocks = channels // LANES
    embed = proj.shape[1]
    dp, space = lax.axis_size("dp"), lax.axis_size("space")
    tall = rows + 2 * reach
    share = -(-blocks // dp)
    owned = -(-side // space)
    parts = (dp, share, space * owned, side, LANES)
    vmem = pl.BlockSpec(memory_space=pltpu.VMEM)
    hbm = pl.BlockSpec(memory_space=pltpu.HBM)
    dma = pltpu.SemaphoreType.DMA
    scratch = [
        pltpu.VMEM((rows, cols, channels), jnp.bfloat16),
        pltpu.VMEM(dw_kernel.shape, dw_kernel.dtype),
        pltpu.VMEM((1, channels), f32),
        pltpu.VMEM((1, channels), f32),
        pltpu.VMEM((1, channels), f32),
        pltpu.VMEM((1, embed), f32),
        pltpu.VMEM((blocks, reach, cols, LANES), jnp.bfloat16),
        pltpu.VMEM((blocks, reach, cols, LANES), jnp.bfloat16),
        pltpu.VMEM((blocks, tall, cols, LANES), f32),
        pltpu.VMEM((tall, cols, LANES), f32),
        pltpu.VMEM((tall, cols, LANES), f32),
        pltpu.VMEM((tall, cols + 2 * PAD, LANES), f32),
        pltpu.VMEM((tall, cols + 2 * PAD, LANES), f32),
        pltpu.VMEM((taps, 8, LANES), f32),
        pltpu.VMEM((1, channels), f32),
        pltpu.VMEM((blocks, 8, LANES), f32),
        pltpu.VMEM((blocks, 8, LANES), f32),
        pltpu.VMEM(proj.shape, proj.dtype),
        pltpu.VMEM(proj.shape[::-1], proj.dtype),
        pltpu.VMEM((space, 1, channels), f32),
        pltpu.VMEM((dp, 1, embed), f32),
        pltpu.VMEM((dp, 1, embed), f32),
        pltpu.VMEM(parts, f32),
        pltpu.VMEM(parts, f32),
        pltpu.VMEM(parts[1:], f32),
        pltpu.VMEM((space, share, owned, side, LANES), f32),
        dma((7,)),
        dma((4, blocks)),
        dma((4, 2)),
    ]
    for shape in ((space,), (dp,), (dp,), (dp, share), (space,), (space,), (dp,)):
        scratch += [dma(shape), dma(shape)]
    grad_images, summed, loss, text_grad = pl.pallas_call(
        functools.partial(block_kernel, side, rows * space * cols),
        in_specs=[hbm] * 7 + [
                               pl.BlockSpec(memory_space=pltpu.SMEM)],
        out_specs=[vmem] * 4,
        out_shape=[
            jax.ShapeDtypeStruct((rows, cols, channels), jnp.bfloat16),
            jax.ShapeDtypeStruct(parts, f32),
            jax.ShapeDtypeStruct((1, 1), f32),
            jax.ShapeDtypeStruct((1, embed), f32),
        ],
        scratch_shapes=scratch,
        compiler_params=pltpu.CompilerParams(
            collective_id=0, has_side_effects=True, vmem_limit_bytes=VMEM_LIMIT
        ),
        name="block",
    )(images[0], dw_kernel, dw_bias, ln_gain, ln_shift, proj, text, logit_scale)
    summed = summed.reshape(dp * share, space * owned, side, LANES)[:blocks, :side]
    kernel_grad = jnp.transpose(summed, (1, 2, 0, 3)).reshape(side, side, channels)
    return loss.reshape(()), grad_images[None], kernel_grad, text_grad


def solution(mesh):
    placed = (P("dp", "space", None, None), P(), P(), P(), P(), P(), P("dp", None), P())
    return jax.shard_map(
        shards,
        mesh=mesh,
        in_specs=placed,
        out_specs=(P(), P("dp", "space", None, None), P(), P("dp", None)),
        check_vma=False,
    )
```

```python
import functools

import jax
import jax.numpy as jnp
from jax import lax
from jax.experimental import pallas as pl
from jax.experimental.pallas import tpu as pltpu
from jax.sharding import PartitionSpec as P

LANES = 128
PAD = 8
TILE = 32
VMEM_LIMIT = 50 * 1024 * 1024
MESH = pl.DeviceIdType.MESH


def fill_taps(taps_ref, k_ref, lanes):
    side = k_ref.shape[0]
    for a in range(side):
        rows = k_ref[a, :, lanes].astype(jnp.float32)
        for d in range(side):
            taps_ref[a * side + d] = jnp.broadcast_to(rows[d : d + 1, :], taps_ref.shape[1:])


def fill_padded(pad_ref, parts, cols):
    first = 0
    for part in parts:
        pad_ref[first : first + part.shape[0], PAD : PAD + cols, :] = part.astype(jnp.float32)
        first += part.shape[0]


def clear_edges(pad_ref, cols):
    rows = pad_ref.shape[0]
    zeros = jnp.zeros((rows, PAD, LANES), jnp.float32)
    pad_ref[:, 0:PAD, :] = zeros
    pad_ref[:, PAD + cols : PAD + cols + PAD, :] = zeros


def convolve(pad_ref, taps_ref, side, rows, start, flip):
    reach = side // 2
    acc = [None] * rows
    for r in range(rows + side - 1):
        for d in range(side):
            first = PAD - reach + d + start
            x = pad_ref[r, first : first + TILE, :].reshape(TILE // 8, 8, LANES)
            for a in range(side):
                h = r - a
                if 0 <= h < rows:
                    tap = (side - 1 - a) * side + side - 1 - d if flip else a * side + d
                    product = x * taps_ref[tap][None]
                    acc[h] = product if acc[h] is None else acc[h] + product
    return acc


def entry_barrier(names):
    barrier = pltpu.get_barrier_semaphore()
    count = 0
    for name in names:
        size = lax.axis_size(name)
        me = lax.axis_index(name)
        for j in range(1, size):
            pl.semaphore_signal(
                barrier, inc=1, device_id={name: lax.rem(me + j, size)}, device_id_type=MESH
            )
        count += size - 1
    pl.semaphore_wait(barrier, count)


def swap(name, source, target, send_sem, recv_sem):
    size = lax.axis_size(name)
    me = lax.axis_index(name)
    copies = []
    for j in range(1, size):
        peer = lax.rem(me + j, size)
        copies.append(pltpu.make_async_remote_copy(
            src_ref=source(peer),
            dst_ref=target(j),
            send_sem=send_sem.at[j],
            recv_sem=recv_sem.at[j],
            device_id={name: peer},
            device_id_type=MESH,
        ))
    return copies


def start_all(copies):
    for copy in copies:
        copy.start()


def exchange(*args):
    copies = swap(*args)
    start_all(copies)
    return copies


def wait_all(copies):
    for copy in copies:
        copy.wait()


def split3(row):
    one = row.astype(jnp.bfloat16)
    rest = row - one.astype(jnp.float32)
    two = rest.astype(jnp.bfloat16)
    three = (rest - two.astype(jnp.float32)).astype(jnp.bfloat16)
    return jnp.concatenate(
        [one, two, three, jnp.zeros((13, row.shape[1]), jnp.bfloat16)], axis=0
    )


def logsum(scores, axis):
    highest = jnp.max(scores, axis=axis, keepdims=True)
    return highest + jnp.log(jnp.sum(jnp.exp(scores - highest), axis=axis, keepdims=True))


def lanes_of(b):
    return pl.ds(pl.multiple_of(b * LANES, LANES), LANES)


def block_kernel(side, pixel_count,
                 image_hbm, k_hbm, bias_hbm, gain_hbm, shift_hbm, proj_hbm, text_hbm, scale_ref,
                 grad_ref, sum_ref, loss_ref, text_grad_ref,
                 image_ref, k_ref, bias_ref, gain_ref, shift_ref, text_ref, low_ref, high_ref, normed_ref, inv_ref, coef_ref, pad_ref, gpad_ref, taps_ref,
                 pool_ref, weight_ref, centred_ref, proj_ref, turned_ref, pools_ref, txts_ref, imgs_ref,
                 part_ref, dp_ref, mine_ref, space_ref,
                 local_sems, image_sems, wide_sems, *sems):
    rows, cols, channels = image_hbm.shape
    blocks = channels // LANES
    reach = side // 2
    dp, space = lax.axis_size("dp"), lax.axis_size("space")
    me, mine = lax.axis_index("dp"), lax.axis_index("space")
    has_low, has_high = mine > 0, mine < space - 1
    share, owned = part_ref.shape[1], part_ref.shape[2] // space

    image_copy = pltpu.make_async_copy(image_hbm, image_ref, local_sems.at[0])
    bias_copy = pltpu.make_async_copy(bias_hbm, bias_ref.at[0], local_sems.at[1])
    gain_copy = pltpu.make_async_copy(gain_hbm, gain_ref.at[0], local_sems.at[2])
    shift_copy = pltpu.make_async_copy(shift_hbm, shift_ref.at[0], local_sems.at[3])
    proj_copy = pltpu.make_async_copy(proj_hbm, proj_ref, local_sems.at[4])
    text_copy = pltpu.make_async_copy(text_hbm, text_ref, local_sems.at[5])
    k_copy = pltpu.make_async_copy(k_hbm, k_ref, local_sems.at[6])
    start_all([text_copy, image_copy, k_copy, bias_copy, gain_copy, shift_copy, proj_copy])
    entry_barrier(("dp", "space"))

    def to_high(b):
        return pltpu.make_async_remote_copy(
            src_ref=image_hbm.at[rows - reach : rows, :, lanes_of(b)], dst_ref=low_ref.at[b],
            send_sem=image_sems.at[0, b], recv_sem=image_sems.at[1, b],
            device_id={"space": mine + 1}, device_id_type=MESH,
        )

    def to_low(b):
        return pltpu.make_async_remote_copy(
            src_ref=image_hbm.at[0:reach, :, lanes_of(b)], dst_ref=high_ref.at[b],
            send_sem=image_sems.at[2, b], recv_sem=image_sems.at[3, b],
            device_id={"space": mine - 1}, device_id_type=MESH,
        )

    def send_image(b, carry):
        @pl.when(has_high)
        def _():
            to_high(b).start()

        @pl.when(has_low)
        def _():
            to_low(b).start()

        return carry

    lax.fori_loop(0, blocks, send_image, 0)

    @pl.when(jnp.logical_not(has_low))
    def _():
        low_ref[...] = jnp.zeros_like(low_ref)
        normed_ref[:, 0:reach] = jnp.zeros((blocks, reach, cols, LANES), jnp.float32)
        inv_ref[0:reach] = jnp.zeros((reach, cols, LANES), jnp.float32)

    @pl.when(jnp.logical_not(has_high))
    def _():
        high_ref[...] = jnp.zeros_like(high_ref)
        normed_ref[:, reach + rows :] = jnp.zeros((blocks, reach, cols, LANES), jnp.float32)
        inv_ref[reach + rows :] = jnp.zeros((reach, cols, LANES), jnp.float32)

    text_copy.wait()
    text = text_ref[...]
    text_norm = jnp.sqrt(jnp.sum(text * text, axis=1, keepdims=True))
    unit_txt = text / text_norm
    txts_ref[me] = unit_txt
    txt_copies = exchange(
        "dp", lambda p: txts_ref.at[me], lambda j: txts_ref.at[me], sems[2], sems[3]
    )
    clear_edges(pad_ref, cols)
    clear_edges(gpad_ref, cols)
    proj_copy.wait()
    for b in range(blocks):
        span = slice(b * LANES, (b + 1) * LANES)
        turned_ref[:, span] = proj_ref[span, :].T
    wait_all([image_copy, k_copy, bias_copy, gain_copy, shift_copy])

    def forward(b, carry):
        fill_taps(taps_ref, k_ref, lanes_of(b))

        @pl.when(has_low)
        def _():
            to_high(b).wait_recv()

        @pl.when(has_high)
        def _():
            to_low(b).wait_recv()

        fill_padded(pad_ref, (low_ref[b], image_ref[:, :, lanes_of(b)], high_ref[b]), cols)
        bias = bias_ref[:, lanes_of(b)]
        for start in range(0, cols, TILE):
            acc = convolve(pad_ref, taps_ref, side, rows, start, False)
            for h in range(rows):
                normed_ref[b, reach + h, start : start + TILE, :] = (
                    acc[h].reshape(TILE, LANES) + bias
                )
        return carry

    lax.fori_loop(0, blocks, forward, 0)

    weight_ref[...] = jnp.zeros_like(weight_ref)

    def normalize(h, carry):
        r = reach + h
        total = normed_ref[0, r]
        for b in range(1, blocks):
            total = total + normed_ref[b, r]
        mu = jnp.sum(total, axis=1, keepdims=True) / channels
        mu = jnp.broadcast_to(mu, (cols, LANES))
        total = None
        for b in range(blocks):
            centred = normed_ref[b, r] - mu
            total = centred * centred if total is None else total + centred * centred
        spread = jnp.sum(total, axis=1, keepdims=True) / channels
        inv = jnp.broadcast_to(lax.rsqrt(spread + 1e-6), (cols, LANES))
        inv_ref[r] = inv
        for b in range(blocks):
            normed = (normed_ref[b, r] - mu) * inv
            normed_ref[b, r] = normed
            weight_ref[b] += jnp.sum(normed.reshape(cols // 8, 8, LANES), axis=0)
        return carry

    lax.fori_loop(0, rows, normalize, 0)
    for b in range(blocks):
        span = slice(b * LANES, (b + 1) * LANES)
        pool_ref[:, span] = (
            jnp.sum(weight_ref[b], axis=0, keepdims=True) * gain_ref[:, span]
            + (rows * cols) * shift_ref[:, span]
        )
    pool_copies = exchange("space", lambda p: pool_ref, lambda j: pools_ref.at[j], sems[0], sems[1])

    def wide(up):
        copies = []
        for i, ref in enumerate((normed_ref, inv_ref)):
            cut = (lambda a, z: ref.at[:, a:z]) if i == 0 else (lambda a, z: ref.at[a:z])
            source = cut(rows, rows + reach) if up else cut(reach, 2 * reach)
            target = cut(0, reach) if up else cut(rows + reach, rows + 2 * reach)
            copies.append(pltpu.make_async_remote_copy(
                src_ref=source, dst_ref=target,
                send_sem=wide_sems.at[0 if up else 2, i], recv_sem=wide_sems.at[1 if up else 3, i],
                device_id={"space": mine + 1 if up else mine - 1}, device_id_type=MESH,
            ))
        return copies

    wait_all(pool_copies)

    @pl.when(has_high)
    def _():
        for copy in wide(True):
            copy.start()

    @pl.when(has_low)
    def _():
        for copy in wide(False):
            copy.start()

    pools_ref[0] = pool_ref[...]
    pooled = None
    for s in range(space):
        term = pools_ref[lax.rem(mine - s + space, space)]
        pooled = term if pooled is None else pooled + term
    pooled = pooled / pixel_count
    embedded = jnp.sum(
        jnp.dot(split3(pooled), proj_ref[...], preferred_element_type=jnp.float32),
        axis=0, keepdims=True,
    )
    emb_norm = jnp.sqrt(jnp.sum(embedded * embedded, axis=1, keepdims=True))
    unit_img = embedded / emb_norm
    imgs_ref[me] = unit_img
    img_copies = exchange(
        "dp", lambda p: imgs_ref.at[me], lambda j: imgs_ref.at[me], sems[4], sems[5]
    )
    wait_all(txt_copies)
    wait_all(img_copies)
    imgs = jnp.concatenate([imgs_ref[i] for i in range(dp)], axis=0)
    txts = jnp.concatenate([txts_ref[i] for i in range(dp)], axis=0)
    factor = scale_ref[0]
    row_id = lax.broadcasted_iota(jnp.int32, (dp, dp), 0)
    col_id = lax.broadcasted_iota(jnp.int32, (dp, dp), 1)
    scores = jnp.zeros((dp, dp), jnp.float32)
    turned = jnp.zeros((dp, dp), jnp.float32)
    for i in range(dp):
        column = factor * jnp.sum(imgs * txts[i : i + 1], axis=1, keepdims=True)
        scores = jnp.where(col_id == i, column, scores)
        column = factor * jnp.sum(txts * imgs[i : i + 1], axis=1, keepdims=True)
        turned = jnp.where(col_id == i, column, turned)
    identity = (row_id == col_id).astype(jnp.float32)
    row_ls, col_ls = logsum(scores, 1), logsum(scores, 0)
    trow_ls, tcol_ls = logsum(turned, 1), logsum(turned, 0)
    diagonal = jnp.sum(scores * identity, axis=1, keepdims=True)
    tdiagonal = jnp.sum(turned * identity, axis=1, keepdims=True)
    loss = jnp.sum(row_ls - diagonal, axis=0, keepdims=True) + jnp.sum(
        trow_ls - tdiagonal, axis=0, keepdims=True
    )
    loss_ref[...] = loss / (2 * dp)
    grad = 0.5 * (jnp.exp(scores - row_ls) + jnp.exp(scores - col_ls)) - identity
    tgrad = 0.5 * (jnp.exp(turned - trow_ls) + jnp.exp(turned - tcol_ls)) - identity
    own = (col_id == me).astype(jnp.float32)
    own_img = jnp.sum(tgrad * own, axis=1, keepdims=True)
    own_txt = jnp.sum(grad * own, axis=1, keepdims=True)
    unit_img_grad = factor * jnp.sum(own_img * txts, axis=0, keepdims=True)
    unit_txt_grad = factor * jnp.sum(own_txt * imgs, axis=0, keepdims=True)
    text_grad_ref[...] = (
        unit_txt_grad - unit_txt * jnp.sum(unit_txt * unit_txt_grad, axis=1, keepdims=True)
    ) / text_norm
    emb_grad = (
        unit_img_grad - unit_img * jnp.sum(unit_img * unit_img_grad, axis=1, keepdims=True)
    ) / emb_norm
    back = jnp.dot(split3(emb_grad), turned_ref[...], preferred_element_type=jnp.float32)
    weighted = jnp.sum(back, axis=0, keepdims=True) * gain_ref[...]
    weight_mean = jnp.sum(weighted, axis=1, keepdims=True) / channels
    for b in range(blocks):
        row = weighted[:, b * LANES : (b + 1) * LANES]
        weight_ref[b] = jnp.broadcast_to(row, (8, LANES))
        centred_ref[b] = jnp.broadcast_to(row - weight_mean, (8, LANES))

    def fill_coef(r, carry):
        total = None
        for b in range(blocks):
            term = normed_ref[b, r].reshape(cols // 8, 8, LANES) * weight_ref[b][None]
            total = term if total is None else total + term
        mean = jnp.sum(total.reshape(cols, LANES), axis=1, keepdims=True) / channels
        coef_ref[r] = inv_ref[r] * jnp.broadcast_to(mean, (cols, LANES))
        return carry

    def fill_grad(b, first, last):
        for r in range(first, last):
            base = (inv_ref[r].reshape(cols // 8, 8, LANES) * centred_ref[b][None]).reshape(
                cols, LANES
            )
            gpad_ref[r, PAD : PAD + cols, :] = base - normed_ref[b, r] * coef_ref[r]

    lax.fori_loop(reach, reach + rows, fill_coef, 0)
    part_ref[...] = jnp.zeros_like(part_ref)

    def piece(owner, k, j):
        return pltpu.make_async_remote_copy(
            src_ref=part_ref.at[owner, k], dst_ref=dp_ref.at[j, k],
            send_sem=sems[6].at[j, k], recv_sem=sems[7].at[j, k],
            device_id={"dp": owner}, device_id_type=MESH,
        )

    def to_owner(b):
        return piece(b // share, b % share, lax.rem(b // share - me + dp, dp))

    def kernel_terms(b, carry):
        fill_padded(pad_ref, (low_ref[b], image_ref[:, :, lanes_of(b)], high_ref[b]), cols)
        fill_grad(b, reach, reach + rows)
        for d in range(side):
            acc = [None] * side
            for w in range(0, cols, 8):
                own = [gpad_ref[reach + h, PAD + w : PAD + w + 8, :] for h in range(rows)]
                for r in range(rows + side - 1):
                    x = pad_ref[r, PAD - reach + d + w : PAD - reach + d + w + 8, :]
                    for a in range(side):
                        h = r - a
                        if 0 <= h < rows:
                            product = x * own[h]
                            acc[a] = product if acc[a] is None else acc[a] + product
            for a in range(side):
                part_ref[b // share, b % share, a, d : d + 1, :] = jnp.sum(
                    acc[a], axis=0, keepdims=True
                )

        @pl.when(b // share != me)
        def _():
            to_owner(b).start()

        return carry

    lax.fori_loop(0, blocks, kernel_terms, 0)

    def share_space():
        return swap("space", lambda p: mine_ref.at[:, pl.ds(p * owned, owned)],
                    lambda j: space_ref.at[j], sems[8], sems[9])

    def own_piece():
        return sum_ref.at[me, :, pl.ds(mine * owned, owned)]

    def back_space():
        return swap("space", lambda p: own_piece(), lambda j: own_piece(), sems[10], sems[11])

    def back_dp():
        return swap("dp", lambda p: sum_ref.at[me], lambda j: sum_ref.at[me], sems[12], sems[13])

    @pl.when(has_high)
    def _():
        for copy in wide(True):
            copy.wait_send()
        for copy in wide(False):
            copy.wait_recv()

    @pl.when(has_low)
    def _():
        for copy in wide(False):
            copy.wait_send()
        for copy in wide(True):
            copy.wait_recv()

    lax.fori_loop(0, reach, fill_coef, 0)
    lax.fori_loop(reach + rows, rows + 2 * reach, fill_coef, 0)

    def input_grad(b, carry):
        @pl.when(b == 1)
        def _():
            for j in range(1, dp):
                for k in range(share):
                    @pl.when(me * share + k < blocks)
                    def _():
                        piece(lax.rem(me + j, dp), k, j).wait_recv()
            total = part_ref[me]
            for j in range(1, dp):
                total = total + dp_ref[j]
            mine_ref[...] = total
            start_all(share_space())

        @pl.when(b == blocks // 3)
        def _():
            wait_all(share_space())
            total = mine_ref[:, pl.ds(mine * owned, owned)]
            for j in range(1, space):
                total = total + space_ref[j]
            sum_ref[me, :, pl.ds(mine * owned, owned)] = total / pixel_count
            start_all(back_space())

        @pl.when(b == 7 * blocks // 12)
        def _():
            wait_all(back_space())
            start_all(back_dp())

        fill_taps(taps_ref, k_ref, lanes_of(b))
        fill_grad(b, 0, rows + 2 * reach)
        for start in range(0, cols, TILE):
            acc = convolve(gpad_ref, taps_ref, side, rows, start, True)
            for h in range(rows):
                grad_ref[h, start : start + TILE, lanes_of(b)] = (
                    acc[h].reshape(TILE, LANES).astype(grad_ref.dtype)
                )
        return carry

    lax.fori_loop(0, blocks, input_grad, 0)
    wait_all(back_dp())

    def image_sent(b, carry):
        @pl.when(b // share != me)
        def _():
            to_owner(b).wait_send()

        @pl.when(has_high)
        def _():
            to_high(b).wait_send()

        @pl.when(has_low)
        def _():
            to_low(b).wait_send()

        return carry

    lax.fori_loop(0, blocks, image_sent, 0)


def shards(images, dw_kernel, dw_bias, ln_gain, ln_shift, proj, text, logit_scale):
    f32 = jnp.float32
    _, rows, cols, channels = images.shape
    side = dw_kernel.shape[0]
    reach = side // 2
    taps = side * side
    blocks = channels // LANES
    embed = proj.shape[1]
    dp, space = lax.axis_size("dp"), lax.axis_size("space")
    tall = rows + 2 * reach
    share = -(-blocks // dp)
    owned = -(-side // space)
    parts = (dp, share, space * owned, side, LANES)
    vmem = pl.BlockSpec(memory_space=pltpu.VMEM)
    hbm = pl.BlockSpec(memory_space=pltpu.HBM)
    dma = pltpu.SemaphoreType.DMA
    scratch = [
        pltpu.VMEM((rows, cols, channels), jnp.bfloat16),
        pltpu.VMEM(dw_kernel.shape, dw_kernel.dtype),
        pltpu.VMEM((1, channels), f32),
        pltpu.VMEM((1, channels), f32),
        pltpu.VMEM((1, channels), f32),
        pltpu.VMEM((1, embed), f32),
        pltpu.VMEM((blocks, reach, cols, LANES), jnp.bfloat16),
        pltpu.VMEM((blocks, reach, cols, LANES), jnp.bfloat16),
        pltpu.VMEM((blocks, tall, cols, LANES), f32),
        pltpu.VMEM((tall, cols, LANES), f32),
        pltpu.VMEM((tall, cols, LANES), f32),
        pltpu.VMEM((tall, cols + 2 * PAD, LANES), f32),
        pltpu.VMEM((tall, cols + 2 * PAD, LANES), f32),
        pltpu.VMEM((taps, 8, LANES), f32),
        pltpu.VMEM((1, channels), f32),
        pltpu.VMEM((blocks, 8, LANES), f32),
        pltpu.VMEM((blocks, 8, LANES), f32),
        pltpu.VMEM(proj.shape, proj.dtype),
        pltpu.VMEM(proj.shape[::-1], proj.dtype),
        pltpu.VMEM((space, 1, channels), f32),
        pltpu.VMEM((dp, 1, embed), f32),
        pltpu.VMEM((dp, 1, embed), f32),
        pltpu.VMEM(parts, f32),
        pltpu.VMEM(parts, f32),
        pltpu.VMEM(parts[1:], f32),
        pltpu.VMEM((space, share, owned, side, LANES), f32),
        dma((7,)),
        dma((4, blocks)),
        dma((4, 2)),
    ]
    for shape in ((space,), (dp,), (dp,), (dp, share), (space,), (space,), (dp,)):
        scratch += [dma(shape), dma(shape)]
    grad_images, summed, loss, text_grad = pl.pallas_call(
        functools.partial(block_kernel, side, rows * space * cols),
        in_specs=[hbm] * 7 + [
                               pl.BlockSpec(memory_space=pltpu.SMEM)],
        out_specs=[vmem] * 4,
        out_shape=[
            jax.ShapeDtypeStruct((rows, cols, channels), jnp.bfloat16),
            jax.ShapeDtypeStruct(parts, f32),
            jax.ShapeDtypeStruct((1, 1), f32),
            jax.ShapeDtypeStruct((1, embed), f32),
        ],
        scratch_shapes=scratch,
        compiler_params=pltpu.CompilerParams(
            collective_id=0, has_side_effects=True, vmem_limit_bytes=VMEM_LIMIT
        ),
        name="block",
    )(images[0], dw_kernel, dw_bias, ln_gain, ln_shift, proj, text, logit_scale)
    summed = summed.reshape(dp * share, space * owned, side, LANES)[:blocks, :side]
    kernel_grad = jnp.transpose(summed, (1, 2, 0, 3)).reshape(side, side, channels)
    return loss.reshape(()), grad_images[None], kernel_grad, text_grad


def solution(mesh):
    placed = (P("dp", "space", None, None), P(), P(), P(), P(), P(), P("dp", None), P())
    return jax.shard_map(
        shards,
        mesh=mesh,
        in_specs=placed,
        out_specs=(P(), P("dp", "space", None, None), P(), P("dp", None)),
        check_vma=False,
    )
```
